512 devices in a mesh: row: 32 (over x_lo, z, core), aisle: 16 (over y, x_hi).
Axes of the slice: x: 4 (x_hi: 2, x_lo: 2; x = x_hi * 2 + x_lo), y: 8, z: 8, core: 2. Of those that a mesh axis runs over, the one named last changes fastest.
Arguments:
- flow_state: bfloat16 [64, 256, 32, 256], P('row', 'aisle'), may hold values from -6 to 6
- mode_weight: bfloat16 [2, 64, 64, 32, 1024], P(None, 'row', 'aisle'), may hold values from -4 to 4
- bypass_weight: bfloat16 [32, 32], replicated, may hold values from -1 to 1
- bias_term: float32 [32], replicated, may hold values from -1 to 1
Outputs:
- mixed_field: bfloat16 [64, 256, 32, 256], P('row', 'aisle')
The draws below stay inside these ranges and needn't reach their ends.
All inputs are finite; a program needn't handle non-finite values.
Results may differ from the reference program's by a relative error of at most 0.025.
Values may be sent and summed in bfloat16 or wider, within the bound.
A program may use at most 64 MiB of HBM per device.

```python
import math
import jax
import jax.numpy as jnp
from jax import lax

C = 32
MX = 64
MY = 64
MZ = 32
NZ = 256
NX = 64
NY = 256


def levels(rng, extent, pieces, low, top_value):
    level = 1.0
    for position, parts in pieces:
        heights = jax.random.uniform(jax.random.fold_in(jax.random.fold_in(rng, 6), position), (parts,), jnp.float32, low / len(pieces), top_value / len(pieces))
        level = level * jnp.repeat(jnp.exp(heights), extent[position] // parts).reshape((-1,) + (1,) * (len(extent) - 1 - position))
    return level


def centred(own_key, dims, spread, bound, pieces=(), kind=jnp.bfloat16):
    result = spread * jax.random.normal(own_key, dims, jnp.float32)
    if pieces:
        result = result * levels(own_key, dims, pieces, -0.22, 0.18)
    return jnp.clip(result, -bound, bound).astype(kind)


def setup_inputs(seed: int = 0) -> dict:
    splits = jax.random.split(jax.random.key(seed), 5)
    return {
        "flow_state": centred(splits[0], (NX, NY, C, NZ), 1.0, 6.0, ((0, 32), (1, 16))),
        "mode_weight": centred(splits[1], (2, MX, MY, MZ, C * C), 2 ** -0.5, 4.0, ((1, 32), (2, 16))),
        "bypass_weight": centred(splits[2], (C, C), C ** -0.5, 1.0),
        "bias_term": jnp.clip(jax.random.uniform(splits[3], (C,), jnp.float32, -1.0, 1.0), -1.0, 1.0),
    }


def twiddle(frequencies, positions, length):
    phase_index = jnp.mod(frequencies[:, None] * positions[None, :], length).astype(jnp.float32)
    angles = phase_index * (2.0 * math.pi / length)
    return (jnp.cos(angles).astype(jnp.bfloat16), jnp.sin(angles).astype(jnp.bfloat16))

def height_tables(height):
    frequencies = jnp.arange(MZ, dtype=jnp.int32)
    positions = jnp.arange(height, dtype=jnp.int32)
    phase_index = jnp.mod(frequencies[:, None] * positions[None, :], height).astype(jnp.float32)
    angles = phase_index * (2.0 * math.pi / height)
    cos_height = jnp.cos(angles)
    sin_height = jnp.sin(angles)
    forward = jnp.concatenate([cos_height, -sin_height], 0).T.astype(jnp.bfloat16)
    weights = jnp.where(frequencies == 0, 1.0, 2.0).astype(jnp.float32)[:, None]
    inverse = jnp.concatenate([weights * cos_height, -weights * sin_height], 0).astype(jnp.bfloat16)
    return (forward, inverse)

def exact(pattern, left, right):
    return jnp.einsum(pattern, left.astype(jnp.float32), right.astype(jnp.float32), precision=lax.Precision.HIGHEST)

def reference(flow_state, mode_weight, bypass_weight, bias_term):
    forward_z, inverse_z = height_tables(NZ)
    scaling = 1.0 / math.sqrt(NX * NY * NZ)
    z_spectrum = jnp.dot(flow_state.reshape(NX * NY * C, NZ), forward_z, preferred_element_type=jnp.float32)
    z_spectrum = z_spectrum.astype(jnp.bfloat16).reshape(NX, NY, C, 2, MZ)
    cos_y, sin_y = twiddle(jnp.arange(MY, dtype=jnp.int32) - MY // 2, jnp.arange(NY, dtype=jnp.int32), NY)
    z_real = z_spectrum[:, :, :, 0]
    z_imag = z_spectrum[:, :, :, 1]
    pattern = 'qy,xyck->qxck'
    y_real = exact(pattern, cos_y, z_real) + exact(pattern, sin_y, z_imag)
    y_imag = exact(pattern, cos_y, z_imag) - exact(pattern, sin_y, z_real)
    y_sums = jnp.stack([y_real, y_imag], 1).astype(jnp.bfloat16)
    cos_x, sin_x = twiddle(jnp.arange(MX, dtype=jnp.int32) - MX // 2, jnp.arange(NX, dtype=jnp.int32), NX)
    pattern = 'px,qxck->pqck'
    x_real = exact(pattern, cos_x, y_sums[:, 0]) + exact(pattern, sin_x, y_sums[:, 1])
    x_imag = exact(pattern, cos_x, y_sums[:, 1]) - exact(pattern, sin_x, y_sums[:, 0])
    mode_sums = (jnp.stack([x_real, x_imag], 1) * scaling).astype(jnp.bfloat16)

    def mix_row(members):
        sums_row, weight_real, weight_imag = members
        weight_real = weight_real.reshape(MY, MZ, C, C)
        weight_imag = weight_imag.reshape(MY, MZ, C, C)
        pattern_mix = 'qck,qkco->qok'
        mixed_real = exact(pattern_mix, sums_row[0], weight_real) - exact(pattern_mix, sums_row[1], weight_imag)
        mixed_imag = exact(pattern_mix, sums_row[0], weight_imag) + exact(pattern_mix, sums_row[1], weight_real)
        return jnp.stack([mixed_real, mixed_imag], 0).astype(jnp.bfloat16)
    mode_mixed = lax.map(mix_row, (mode_sums, mode_weight[0], mode_weight[1]))
    pattern = 'px,pqok->xqok'
    back_real = exact(pattern, cos_x, mode_mixed[:, 0]) - exact(pattern, sin_x, mode_mixed[:, 1])
    back_imag = exact(pattern, cos_x, mode_mixed[:, 1]) + exact(pattern, sin_x, mode_mixed[:, 0])
    back_x = jnp.stack([back_real, back_imag], 0).astype(jnp.bfloat16)
    pattern = 'qy,xqok->xyok'
    plane_real = exact(pattern, cos_y, back_x[0]) - exact(pattern, sin_y, back_x[1])
    plane_imag = exact(pattern, cos_y, back_x[1]) + exact(pattern, sin_y, back_x[0])
    back_y = jnp.stack([plane_real, plane_imag], 3).astype(jnp.bfloat16)

    def finish(members):
        cell_rows, planes = members
        spectral = jnp.dot(planes.reshape(NY * C, 2 * MZ), inverse_z, preferred_element_type=jnp.float32)
        spectral = spectral.reshape(NY, C, NZ) * scaling
        bypass = exact('yiz,io->yoz', cell_rows, bypass_weight)
        return jax.nn.gelu(spectral + bypass + bias_term[None, :, None]).astype(jnp.bfloat16)
    return lax.map(finish, (flow_state, back_y))
```

```python
import math

import jax
import jax.numpy as jnp
import numpy as np
from jax import lax
from jax.experimental import pallas as pl
from jax.experimental.pallas import tpu as pltpu
from jax.sharding import PartitionSpec as P

C = 32
MX = 64
MY = 64
MZ = 32
NX = 64
NY = 256
NZ = 256
NR = 32
NA = 16
SCALING = 1.0 / math.sqrt(NX * NY * NZ)
BF = jnp.bfloat16
F32 = jnp.float32
MESH = pl.DeviceIdType.MESH


def twiddle(frequencies, positions, length):
    phase = np.mod(frequencies[:, None] * positions[None, :], length).astype(np.float32)
    angles = phase * np.float32(2.0 * math.pi / length)
    return np.cos(angles), np.sin(angles)


def tables():
    cz, sz = twiddle(np.arange(MZ), np.arange(NZ), NZ)
    weight = np.where(np.arange(MZ) == 0, 1.0, 2.0).astype(np.float32)[:, None]
    forward = np.stack([cz, -sz], 0)
    inverse = np.stack([weight * cz, -weight * sz], 0)
    fz = np.zeros((2, 2, NZ, 2, 2, 2, MZ), np.float32)
    iz = np.zeros((2, 2, 2, 2, 2, MZ, NZ), np.float32)
    for x in range(2):
        for c in range(2):
            fz[x, c, :, :, c, x, :] = forward.transpose(2, 0, 1)
            iz[x, c, :, c, x] = inverse
    fz = fz.reshape(4, 256, 256)
    iz = iz.reshape(4, 256, 256)
    eye = np.eye(16, dtype=np.float32)
    perm = np.einsum("ab,cd->acdb", eye, eye).reshape(256, 256)
    cy, sy = twiddle(np.arange(MY) - MY // 2, np.arange(NY), NY)
    ty = np.stack([np.stack([cy, sy]), np.stack([-sy, cy])])
    t1 = ty.reshape(2, 2, 32, 2, NY).transpose(3, 2, 0, 1, 4).reshape(128, 512)
    cx, sx = twiddle(np.arange(MX) - MX // 2, np.arange(NX), NX)
    tx = np.stack([np.stack([cx, sx]), np.stack([-sx, cx])])
    t2 = tx.reshape(2, 2, MX, 32, 2).transpose(2, 0, 4, 3, 1).reshape(128, 128)
    bx = np.stack([np.stack([cx, -sx]), np.stack([sx, cx])])
    t3 = bx.reshape(2, 2, MX, 32, 2).transpose(4, 3, 0, 2, 1).reshape(128, 128)
    by = np.stack([np.stack([cy, -sy]), np.stack([sy, cy])])
    t4 = by.reshape(2, 2, 32, 2, NY).transpose(0, 4, 3, 2, 1).reshape(512, 128)
    spread = np.einsum("ab,cd,o->acdbo", eye, np.eye(4), np.ones(32)).reshape(64, 2048)
    fold = np.einsum("lm,ab,cd,g->lacdgmb", np.eye(2), eye, np.eye(4), np.ones(4)).reshape(128, 512)
    return [jnp.asarray(t, BF) for t in (fz, perm, t1, t2, spread, fold, t3, t4, iz)]


def dot(left, right):
    return jnp.dot(left, right, preferred_element_type=F32)


def dot_tn(left, right):
    return lax.dot_general(left, right, (((0,), (0,)), ((), ())), preferred_element_type=F32)


def dot_nt(left, right):
    return lax.dot_general(left, right, (((1,), (1,)), ((), ())), preferred_element_type=F32)


def exchange_halves(first, second, roll):
    low = (lax.broadcasted_iota(jnp.int32, first.shape, 1) & 32) == 0
    return (
        jnp.where(low, first, roll(second, 32, 1)),
        jnp.where(low, roll(first, 96, 1), second),
    )


def stage_z(flow, fz, perm):
    total = None
    for x in range(2):
        for c in range(2):
            part = dot(flow[x, :, c * 16 : c * 16 + 16, :].reshape(256, 256), fz[2 * x + c])
            total = part if total is None else total + part
    return dot(perm, total.astype(BF)).astype(BF)


def stage_y(gathered, t1, roll):
    sums = dot(t1, jnp.concatenate([gathered[:, :128], gathered[:, 128:]], 0))
    return exchange_halves(sums[:64], sums[64:], roll)


def stage_mix(modes, spread, fold, weight):
    planes = []
    for p in range(2):
        wide = dot_tn(modes, spread[:, p * 1024 : p * 1024 + 1024])
        real = [None, None]
        imag = [None, None]
        for q in range(2):
            for c in range(2):
                rows = slice(c * 64 + q * 32, c * 64 + q * 32 + 32)
                for h in range(4):
                    mr = wide[rows, h * 128 : h * 128 + 128]
                    mi = wide[rows, 512 + h * 128 : 512 + h * 128 + 128]
                    wr = weight(0, p, q, c * 512 + h * 128).astype(F32)
                    wi = weight(1, p, q, c * 512 + h * 128).astype(F32)
                    re = mr * wr - mi * wi
                    im = mr * wi + mi * wr
                    real[q] = re if real[q] is None else real[q] + re
                    imag[q] = im if imag[q] is None else imag[q] + im
        planes += [jnp.concatenate(real, 0), jnp.concatenate(imag, 0)]
    total = jnp.concatenate(planes, 1)
    high = total.astype(BF)
    low = (total - high.astype(F32)).astype(BF)
    mixed = dot_nt(fold, high) + dot_nt(fold, low)
    return jnp.concatenate([mixed[:64], mixed[64:]], 1)


def stage_y_back(first, second, t4, roll):
    low, high = exchange_halves(first.astype(F32), second.astype(F32), roll)
    return dot(t4, jnp.concatenate([low, high], 0).astype(BF))


def bypass_matrix(bypass, lanes):
    wide = dot(bypass, lanes).astype(BF)
    tall = jnp.concatenate([wide] * 8, 0)
    rows = lax.broadcasted_iota(jnp.int32, (256, 256), 0) // 32
    columns = lax.broadcasted_iota(jnp.int32, (256, 256), 1) // 32
    return jnp.where(rows == columns, tall, jnp.zeros_like(tall))


def stage_z_back(planes, perm, iz, bypass, store):
    rows = dot(perm, planes).astype(BF)
    for x in range(2):
        for o in range(2):
            spectral = dot(rows, iz[2 * x + o]) * SCALING
            total = spectral.reshape(16, 16, 256) + bypass(x, o)
            store(x, o, jax.nn.gelu(total).astype(BF))


def kernel(
    flow, weight, bypass, bias, fz, perm, t1, t2, spread, fold, t3, t4, iz,
    out,
    send_a, recv_a, send_b, recv_b, send_c, recv_c, send_d, recv_d, send_e, recv_e, send_f, recv_f,
    plain, send_sem, recv_sem, own_sem,
):
    row = lax.axis_index("row")
    aisle = lax.axis_index("aisle")
    quad = row // 2
    half = row % 2
    barrier = pltpu.get_barrier_semaphore()

    @pl.loop(1, NA)
    def _(i):
        pl.semaphore_signal(barrier, inc=1, device_id=(row, lax.rem(aisle + i, NA)), device_id_type=MESH)

    @pl.loop(1, NR)
    def _(i):
        pl.semaphore_signal(barrier, inc=1, device_id=(lax.rem(row + i, NR), aisle), device_id_type=MESH)

    send_a[...] = stage_z(flow, fz, perm[...]).reshape(16, 16, 256)
    pl.semaphore_wait(barrier, NA - 1 + NR - 1)

    def remote(stage, source, target, device):
        pltpu.make_async_remote_copy(
            src_ref=source,
            dst_ref=target,
            send_sem=send_sem.at[stage],
            recv_sem=recv_sem.at[stage],
            device_id=device,
            device_id_type=MESH,
        ).start()

    def local(stage, source, target):
        pltpu.make_async_copy(source, target, recv_sem.at[stage]).start()

    def arrived(stage, whole):
        pltpu.make_async_copy(whole, whole, recv_sem.at[stage]).wait()

    def sent(stage, part):
        pltpu.make_async_copy(part, part, send_sem.at[stage]).wait()

    local(0, send_a.at[aisle], recv_a.at[aisle])

    @pl.loop(1, NA)
    def _(i):
        to = lax.rem(aisle + i, NA)
        remote(0, send_a.at[to], recv_a.at[aisle], (row, to))

    lanes = (
        lax.broadcasted_iota(jnp.int32, (32, 256), 0)
        == lax.broadcasted_iota(jnp.int32, (32, 256), 1) % 32
    ).astype(F32).astype(BF)
    diagonal = bypass_matrix(bypass[...], lanes)
    eye = lax.broadcasted_iota(jnp.int32, (32, 32), 0) == lax.broadcasted_iota(jnp.int32, (32, 32), 1)
    column = jnp.sum(jnp.where(eye, bias[...], 0.0), axis=1, keepdims=True)
    tall = jnp.concatenate([column] * 8, 0)
    for x in range(2):
        for y in range(2):
            field = flow[x, y * 8 : y * 8 + 8].reshape(256, 256)
            plain[x, y * 8 : y * 8 + 8] = (dot_tn(diagonal, field) + tall).reshape(8, 32, 256)

    arrived(0, recv_a)
    first, second = stage_y(recv_a[...].reshape(256, 256), t1[...], pltpu.roll)
    send_b.reshape(128, 128)[:64] = first.astype(BF)
    send_b.reshape(128, 128)[64:] = second.astype(BF)

    local(1, send_b.at[:, row], recv_b.at[:, row])

    @pl.loop(1, NR)
    def _(i):
        to = lax.rem(row + i, NR)
        remote(1, send_b.at[:, to], recv_b.at[:, row], (to, aisle))

    arrived(1, recv_b)
    modes = dot(t2[...], recv_b.reshape(128, 128)[...]) * SCALING
    send_c.reshape(128, 128)[...] = modes.astype(BF)

    mine = quad == aisle
    slot = half * 16 + aisle

    @pl.when(mine)
    def _():
        local(2, send_c.at[row], recv_c.at[slot])

    @pl.when(jnp.logical_not(mine))
    def _():
        pltpu.make_async_remote_copy(
            src_ref=send_c.at[row],
            dst_ref=recv_c.at[slot],
            send_sem=own_sem,
            recv_sem=recv_sem.at[2],
            device_id=(row, quad),
            device_id_type=MESH,
        ).start()

    @pl.loop(1, NR)
    def _(i):
        to = lax.rem(row + i, NR)
        remote(2, send_c.at[to], recv_c.at[slot], (to, quad))

    arrived(2, recv_c)

    @pl.when(jnp.logical_not(mine))
    def _():
        pltpu.make_async_copy(send_c.at[0], send_c.at[0], own_sem).wait()

    modes = recv_c.reshape(128, 128)[...]
    for h in range(2):
        mixed = stage_mix(
            modes[h * 64 : h * 64 + 64],
            spread,
            fold[...],
            lambda r, p, q, lane: weight[r, p, 2 * h + q, :, lane : lane + 128],
        )
        send_d.reshape(128, 128)[h * 64 : h * 64 + 64] = mixed.astype(BF)

    home = 2 * aisle
    own = (row - home) * 16 + aisle

    @pl.loop(0, 32)
    def _(i):
        h = i // 16
        to = i % 16
        target_row = home + h
        same = jnp.logical_and(target_row == row, to == aisle)

        @pl.when(same)
        def _():
            local(3, send_d.at[i], recv_d.at[row])

        @pl.when(jnp.logical_not(same))
        def _():
            remote(3, send_d.at[i], recv_d.at[row], (target_row, to))

    arrived(3, recv_d)
    back = dot(t3[...], recv_d.reshape(128, 128)[...])
    send_e.reshape(128, 128)[...] = back.astype(BF)

    local(4, send_e.at[:, row], recv_e.at[:, row])

    @pl.loop(1, NR)
    def _(i):
        to = lax.rem(row + i, NR)
        remote(4, send_e.at[:, to], recv_e.at[:, row], (to, aisle))

    arrived(4, recv_e)
    whole = recv_e.reshape(128, 128)[...]
    back = stage_y_back(whole[:64], whole[64:], t4[...], pltpu.roll).astype(BF)
    for r in range(2):
        send_f[:, r] = back[r * 256 : r * 256 + 256].reshape(16, 16, 128)

    local(5, send_f.at[aisle], recv_f.at[aisle])

    @pl.loop(1, NA)
    def _(i):
        to = lax.rem(aisle + i, NA)
        remote(5, send_f.at[to], recv_f.at[aisle], (row, to))

    arrived(5, recv_f)
    planes = jnp.concatenate(
        [recv_f[:, 0].reshape(256, 128), recv_f[:, 1].reshape(256, 128)], 1
    )

    def store(x, o, value):
        out[x, :, o * 16 : o * 16 + 16, :] = value

    stage_z_back(
        planes, perm[...], iz, lambda x, o: plain[x, :, o * 16 : o * 16 + 16, :], store
    )

    sent(0, send_a.at[pl.ds(0, NA - 1)])
    sent(1, send_b.at[:, pl.ds(0, NR - 1)])
    sent(2, send_c.at[pl.ds(0, NR - 1)])
    sent(4, send_e.at[:, pl.ds(0, NR - 1)])
    sent(5, send_f.at[pl.ds(0, NA - 1)])

    @pl.when(mine)
    def _():
        sent(3, send_d.at[pl.ds(0, 31)])

    @pl.when(jnp.logical_not(mine))
    def _():
        sent(3, send_d)


def on_device(flow_state, mode_weight, bypass_weight, bias_term):
    vmem = pl.BlockSpec(memory_space=pltpu.VMEM)
    pair = lambda *shape: [pltpu.VMEM(shape, BF)] * 2
    return pl.pallas_call(
        kernel,
        out_shape=jax.ShapeDtypeStruct(flow_state.shape, BF),
        in_specs=[vmem] * 13,
        out_specs=vmem,
        scratch_shapes=[
            *pair(16, 16, 256),
            *pair(2, 32, 2, 128),
            *pair(32, 4, 128),
            *pair(32, 4, 128),
            *pair(2, 32, 2, 128),
            *pair(16, 2, 16, 128),
            pltpu.VMEM((2, 16, 32, 256), F32),
            pltpu.SemaphoreType.DMA((6,)),
            pltpu.SemaphoreType.DMA((6,)),
            pltpu.SemaphoreType.DMA,
        ],
        compiler_params=pltpu.CompilerParams(
            collective_id=0, has_side_effects=True, vmem_limit_bytes=40 * 2**20
        ),
        name="fourier_layer",
    )(flow_state, mode_weight, bypass_weight, bias_term.reshape(1, C), *tables())


def solution(mesh):
    in_specs = (P("row", "aisle", None, None), P(None, "row", "aisle", None, None), P(), P())
    return jax.shard_map(
        on_device,
        mesh=mesh,
        in_specs=in_specs,
        out_specs=P("row", "aisle", None, None),
        check_vma=False,
    )
```

```python
import math

import jax
import jax.numpy as jnp
import numpy as np
from jax import lax
from jax.experimental import pallas as pl
from jax.experimental.pallas import tpu as pltpu
from jax.sharding import PartitionSpec as P

C = 32
MX = 64
MY = 64
MZ = 32
NX = 64
NY = 256
NZ = 256
NR = 32
NA = 16
SCALING = 1.0 / math.sqrt(NX * NY * NZ)
BF = jnp.bfloat16
F32 = jnp.float32
MESH = pl.DeviceIdType.MESH


def twiddle(frequencies, positions, length):
    phase = np.mod(frequencies[:, None] * positions[None, :], length).astype(np.float32)
    angles = phase * np.float32(2.0 * math.pi / length)
    return np.cos(angles), np.sin(angles)


def tables():
    cz, sz = twiddle(np.arange(MZ), np.arange(NZ), NZ)
    weight = np.where(np.arange(MZ) == 0, 1.0, 2.0).astype(np.float32)[:, None]
    forward = np.stack([cz, -sz], 0)
    inverse = np.stack([weight * cz, -weight * sz], 0)
    fz = np.zeros((2, 2, NZ, 2, 2, 2, MZ), np.float32)
    iz = np.zeros((2, 2, 2, 2, 2, MZ, NZ), np.float32)
    for x in range(2):
        for c in range(2):
            fz[x, c, :, :, c, x, :] = forward.transpose(2, 0, 1)
            iz[x, c, :, c, x] = inverse
    fz = fz.reshape(4, 256, 256)
    iz = iz.reshape(4, 256, 256)
    eye = np.eye(16, dtype=np.float32)
    perm = np.einsum("ab,cd->acdb", eye, eye).reshape(256, 256)
    cy, sy = twiddle(np.arange(MY) - MY // 2, np.arange(NY), NY)
    ty = np.stack([np.stack([cy, sy]), np.stack([-sy, cy])])
    t1 = ty.reshape(2, 2, 32, 2, 2, 128).transpose(4, 3, 2, 0, 1, 5).reshape(256, 256)
    cx, sx = twiddle(np.arange(MX) - MX // 2, np.arange(NX), NX)
    tx = np.stack([np.stack([cx, sx]), np.stack([-sx, cx])])
    t2 = tx.reshape(2, 2, MX, 32, 2).transpose(2, 0, 4, 3, 1).reshape(128, 128)
    bx = np.stack([np.stack([cx, -sx]), np.stack([sx, cx])])
    t3 = bx.reshape(2, 2, MX, 32, 2).transpose(4, 3, 0, 2, 1).reshape(128, 128)
    by = np.stack([np.stack([cy, -sy]), np.stack([sy, cy])])
    t4 = by.reshape(2, 2, 32, 2, 2, 128).transpose(0, 5, 4, 3, 2, 1).reshape(256, 256)
    spread = np.einsum("ab,ij,cd,o->iacdbjo", np.eye(8), np.eye(2), np.eye(4), np.ones(32))
    spread = spread.reshape(64, 2048)
    fold = np.einsum("lm,ab,ij,cd,g->liacdgmbj", np.eye(2), np.eye(8), np.eye(2), np.eye(4), np.ones(4))
    fold = fold.reshape(128, 512)
    halves = lambda t: np.concatenate(np.split(t, t.shape[1] // 256, 1), 0)
    packed = [
        fz.reshape(1024, 256),
        perm,
        t1,
        np.concatenate([t2, t3], 1),
        halves(spread),
        halves(fold),
        t4,
        iz.reshape(1024, 256),
    ]
    return jnp.asarray(np.concatenate(packed, 0), BF)


FZ = 0
PERM = 1024
T1 = 1280
T23 = 1536
SPREAD = 1664
FOLD = 2176
T4 = 2432
IZ = 2688
ROWS = 3712
GROUPS = ((FZ, T1), (T1, SPREAD), (SPREAD, T4), (T4, ROWS))


def dot(left, right):
    return jnp.dot(left, right, preferred_element_type=F32)


def dot_tn(left, right):
    return lax.dot_general(left, right, (((0,), (0,)), ((), ())), preferred_element_type=F32)


def dot_nt(left, right):
    return lax.dot_general(left, right, (((1,), (1,)), ((), ())), preferred_element_type=F32)


def exchange_halves(first, second, roll):
    low = (lax.broadcasted_iota(jnp.int32, first.shape, 1) & 32) == 0
    return (
        jnp.where(low, first, roll(second, 32, 1)),
        jnp.where(low, roll(first, 96, 1), second),
    )


def stage_z(flow, fz, perm):
    total = None
    for x in range(2):
        for c in range(2):
            part = dot(flow[x, :, c * 16 : c * 16 + 16, :].reshape(256, 256), fz[2 * x + c])
            total = part if total is None else total + part
    return dot(perm, total.astype(BF)).astype(BF)


def near(place, index):
    return ((index - place + 10) & 7) < 4


def near_tables(place, t1, t4):
    columns = (lax.broadcasted_iota(jnp.int32, (128, 256), 1) >> 5) & 3
    rows = (lax.broadcasted_iota(jnp.int32, (256, 128), 0) >> 5) & 3
    first, second = t1[:128].astype(F32), t1[128:].astype(F32)
    left, right = t4[:, :128].astype(F32), t4[:, 128:].astype(F32)
    return (
        jnp.where(near(place, columns), first, second).astype(BF),
        jnp.where(near(place, rows), left, right).astype(BF),
    )


def stage_y(gathered, t1, roll):
    wide = jnp.concatenate(gathered, 1)
    upper = jnp.concatenate([wide[:, 0:128], wide[:, 256:384]], 1)
    lower = jnp.concatenate([wide[:, 128:256], wide[:, 384:512]], 1)
    sums = dot(t1, jnp.concatenate([upper, lower], 0))
    parts = [
        exchange_halves(sums[:64, c * 128 : c * 128 + 128], sums[64:, c * 128 : c * 128 + 128], roll)
        for c in range(2)
    ]
    return [parts[c][x] for x in range(2) for c in range(2)]


def stage_mix(modes, spread, fold, weight):
    planes = []
    for p in range(2):
        wide = dot_tn(modes, spread[:, p * 1024 : p * 1024 + 1024])
        real = [None, None]
        imag = [None, None]
        for q in range(2):
            for c in range(2):
                rows = slice(c * 64 + q * 32, c * 64 + q * 32 + 32)
                for h in range(4):
                    mr = wide[rows, h * 128 : h * 128 + 128]
                    mi = wide[rows, 512 + h * 128 : 512 + h * 128 + 128]
                    wr = weight(0, p, q, c * 512 + h * 128).astype(F32)
                    wi = weight(1, p, q, c * 512 + h * 128).astype(F32)
                    re = mr * wr - mi * wi
                    im = mr * wi + mi * wr
                    real[q] = re if real[q] is None else real[q] + re
                    imag[q] = im if imag[q] is None else imag[q] + im
        planes += [jnp.concatenate(real, 0), jnp.concatenate(imag, 0)]
    total = jnp.concatenate(planes, 1)
    high = total.astype(BF)
    low = (total - high.astype(F32)).astype(BF)
    mixed = dot_nt(fold, high) + dot_nt(fold, low)
    return jnp.concatenate([mixed[:64], mixed[64:]], 1)


def stage_y_back(parts, t4, roll):
    columns = []
    for o in range(2):
        low, high = exchange_halves(parts[o].astype(F32), parts[2 + o].astype(F32), roll)
        columns.append(jnp.concatenate([low, high], 0).astype(BF))
    return dot(t4, jnp.concatenate(columns, 1))


def bypass_matrix(bypass, lanes):
    wide = dot(bypass, lanes).astype(BF)
    tall = jnp.concatenate([wide] * 8, 0)
    rows = lax.broadcasted_iota(jnp.int32, (256, 256), 0) // 32
    columns = lax.broadcasted_iota(jnp.int32, (256, 256), 1) // 32
    return jnp.where(rows == columns, tall, jnp.zeros_like(tall))


def stage_z_back(planes, perm, iz, bypass, store):
    rows = dot(perm, planes).astype(BF)
    for x in range(2):
        for o in range(2):
            spectral = dot(rows, iz[2 * x + o]) * SCALING
            total = spectral.reshape(16, 16, 256) + bypass(x, o)
            store(x, o, jax.nn.gelu(total).astype(BF))


def stages(
    flow_hbm, weight_hbm, bypass_hbm, bias_hbm, table_hbm,
    out,
    flow, weight, bypass, bias, table,
    send_a, recv_a, send_b, recv_b, send_c, recv_c, send_d, recv_d, send_e, recv_e, send_f, recv_f,
    plain, send_sem, recv_sem, own_sem, load_sem, ending,
):
    row = lax.axis_index("row")
    aisle = lax.axis_index("aisle")
    quad = row // 2
    half = row % 2
    place = aisle // 2
    side = aisle % 2
    group = aisle % 8

    loads = [pltpu.make_async_copy(flow_hbm, flow, load_sem.at[0])]
    for i, (first, last) in enumerate(GROUPS):
        part = pl.ds(first, last - first)
        loads.append(pltpu.make_async_copy(table_hbm.at[part], table.at[part], load_sem.at[i + 1]))
    loads.append(pltpu.make_async_copy(bypass_hbm, bypass, load_sem.at[5]))
    loads.append(pltpu.make_async_copy(bias_hbm, bias, load_sem.at[6]))
    loads.append(pltpu.make_async_copy(weight_hbm, weight, load_sem.at[7]))
    for load in loads:
        load.start()

    barrier = pltpu.get_barrier_semaphore()

    @pl.loop(0, 10)
    def _(i):
        other = ((place + i // 2 + 5) % 8) * 2 + i % 2

        @pl.when(other != aisle)
        def _():
            pl.semaphore_signal(barrier, inc=1, device_id=(row, other), device_id_type=MESH)

    @pl.loop(1, NR)
    def _(i):
        pl.semaphore_signal(barrier, inc=1, device_id=(lax.rem(row + i, NR), aisle), device_id_type=MESH)

    def tile(first, rows=256):
        return table[first : first + rows]

    loads[0].wait()
    loads[1].wait()
    fz = [tile(FZ + 256 * i) for i in range(4)]
    send_a[...] = stage_z(flow, fz, tile(PERM)).reshape(8, 2, 16, 256)
    pl.semaphore_wait(barrier, 9 + NR - 1)

    def remote(stage, source, target, device):
        pltpu.make_async_remote_copy(
            src_ref=source,
            dst_ref=target,
            send_sem=send_sem.at[stage],
            recv_sem=recv_sem.at[stage],
            device_id=device,
            device_id_type=MESH,
        ).start()

    def local(stage, source, target):
        pltpu.make_async_copy(source, target, recv_sem.at[stage]).start()

    def arrived(stage, whole):
        pltpu.make_async_copy(whole, whole, recv_sem.at[stage]).wait()

    def sent(stage, part):
        pltpu.make_async_copy(part, part, send_sem.at[stage]).wait()

    local(0, send_a.at[group], recv_a.at[group])

    @pl.loop(0, 8)
    def _(i):
        to = ((place + 7 + i // 2) % 8) * 2 + i % 2

        @pl.when(to != aisle)
        def _():
            remote(0, send_a.at[to % 8], recv_a.at[group], (row, to))

    ending.append(lambda: sent(0, send_a.at[pl.ds(0, 7)]))

    loads[5].wait()
    loads[6].wait()
    lanes = (
        lax.broadcasted_iota(jnp.int32, (32, 256), 0)
        == lax.broadcasted_iota(jnp.int32, (32, 256), 1) % 32
    ).astype(F32).astype(BF)
    diagonal = bypass_matrix(bypass[...], lanes)
    eye = lax.broadcasted_iota(jnp.int32, (32, 32), 0) == lax.broadcasted_iota(jnp.int32, (32, 32), 1)
    column = jnp.sum(jnp.where(eye, bias[...], 0.0), axis=1, keepdims=True)
    tall = jnp.concatenate([column] * 8, 0)
    for x in range(2):
        for y in range(2):
            field = flow[x, y * 8 : y * 8 + 8].reshape(256, 256)
            plain[x, y * 8 : y * 8 + 8] = (dot_tn(diagonal, field) + tall).reshape(8, 32, 256)

    for i in (2, 3, 4, 7):
        loads[i].wait()
    t1, t4 = near_tables(place, tile(T1), tile(T4))
    arrived(0, recv_a)
    yield
    parts = stage_y([recv_a[:, c].reshape(128, 256) for c in range(2)], t1, pltpu.roll)
    for i in range(4):
        send_b.reshape(256, 128)[i * 64 : i * 64 + 64] = parts[i].astype(BF)

    local(1, send_b.at[:, row], recv_b.at[:, row])

    @pl.loop(1, NR)
    def _(i):
        to = lax.rem(row + i, NR)
        remote(1, send_b.at[:, to], recv_b.at[:, row], (to, aisle))

    ending.append(lambda: sent(1, send_b.at[:, pl.ds(0, NR - 1)]))
    arrived(1, recv_b)
    yield
    whole = recv_b.reshape(256, 128)[...]
    columns = [jnp.concatenate([whole[c * 64 : c * 64 + 64], whole[128 + c * 64 : 192 + c * 64]], 0) for c in range(2)]
    modes = (dot(tile(T23, 128)[:, :128], jnp.concatenate(columns, 1)) * SCALING).astype(BF)
    for c in range(2):
        send_c.reshape(256, 128)[c * 128 : c * 128 + 128] = modes[:, c * 128 : c * 128 + 128]

    mine = quad == aisle
    slot = half * 16 + aisle

    @pl.when(mine)
    def _():
        local(2, send_c.at[:, row], recv_c.at[:, slot])

    @pl.when(jnp.logical_not(mine))
    def _():
        pltpu.make_async_remote_copy(
            src_ref=send_c.at[:, row],
            dst_ref=recv_c.at[:, slot],
            send_sem=own_sem,
            recv_sem=recv_sem.at[2],
            device_id=(row, quad),
            device_id_type=MESH,
        ).start()

    @pl.loop(1, NR)
    def _(i):
        to = lax.rem(row + i, NR)
        remote(2, send_c.at[:, to], recv_c.at[:, slot], (to, quad))

    ending.append(lambda: sent(2, send_c.at[:, pl.ds(0, NR - 1)]))
    @ending.append
    def _():
        @pl.when(jnp.logical_not(mine))
        def _():
            pltpu.make_async_copy(send_c.at[:, 0], send_c.at[:, 0], own_sem).wait()

    arrived(2, recv_c)
    yield

    spread = jnp.concatenate([tile(SPREAD + 64 * i, 64) for i in range(8)], 1)
    fold = jnp.concatenate([tile(FOLD, 128), tile(FOLD + 128, 128)], 1)
    whole = recv_c.reshape(256, 128)[...]
    for h in range(2):
        modes = []
        for c in range(2):
            first = c * 128 + h * 64
            modes.append(whole[first : first + 32].astype(F32) + whole[first + 32 : first + 64].astype(F32))
        mixed = stage_mix(
            jnp.concatenate(modes, 0).astype(BF),
            spread,
            fold,
            lambda r, p, q, lane: weight[r, p, 2 * h + q, :, lane : lane + 128],
        )
        send_d.reshape(128, 128)[h * 64 : h * 64 + 64] = mixed.astype(BF)

    home = 2 * aisle

    @pl.loop(0, 32)
    def _(i):
        h = i // 16
        to = i % 16
        target_row = home + h
        same = jnp.logical_and(target_row == row, to == aisle)

        @pl.when(same)
        def _():
            local(3, send_d.at[h, :, to % 8], recv_d.at[:, row])

        @pl.when(jnp.logical_not(same))
        def _():
            remote(3, send_d.at[h, :, to % 8], recv_d.at[:, row], (target_row, to))

    @ending.append
    def _():
        @pl.when(mine)
        def _():
            sent(3, recv_d.at[:, pl.ds(0, 31)])

        @pl.when(jnp.logical_not(mine))
        def _():
            sent(3, recv_d)

    arrived(3, recv_d)
    yield
    whole = recv_d.reshape(256, 128)[...]
    back = dot(tile(T23, 128)[:, 128:], jnp.concatenate([whole[:128], whole[128:]], 1)).astype(BF)
    for x in range(2):
        for o in range(2):
            i = 2 * x + o
            send_e.reshape(256, 128)[i * 64 : i * 64 + 64] = back[x * 64 : x * 64 + 64, o * 128 : o * 128 + 128]

    local(4, send_e.at[:, row], recv_e.at[:, row])

    @pl.loop(1, NR)
    def _(i):
        to = lax.rem(row + i, NR)
        remote(4, send_e.at[:, to], recv_e.at[:, row], (to, aisle))

    ending.append(lambda: sent(4, send_e.at[:, pl.ds(0, NR - 1)]))
    arrived(4, recv_e)
    yield
    whole = recv_e.reshape(256, 128)[...]
    back = stage_y_back([whole[i * 64 : i * 64 + 64] for i in range(4)], t4, pltpu.roll).astype(BF)
    for r in range(2):
        for o in range(2):
            part = back[r * 128 : r * 128 + 128, o * 128 : o * 128 + 128]
            send_f[:, r, o] = part.reshape(8, 16, 128)

    local(5, send_f.at[group], recv_f.at[group])

    @pl.loop(0, 8)
    def _(i):
        to = ((place + 6 + i // 2) % 8) * 2 + i % 2

        @pl.when(to != aisle)
        def _():
            remote(5, send_f.at[to % 8], recv_f.at[group], (row, to))

    ending.append(lambda: sent(5, send_f.at[pl.ds(0, 7)]))
    arrived(5, recv_f)
    yield
    planes = jnp.concatenate(
        [recv_f[:, 0].reshape(256, 128), recv_f[:, 1].reshape(256, 128)], 1
    )

    iz = [tile(IZ + 256 * i) for i in range(4)]

    def store(x, o, value):
        out[x, :, o * 16 : o * 16 + 16, :] = value

    stage_z_back(
        planes, tile(PERM), iz, lambda x, o: plain[x, :, o * 16 : o * 16 + 16, :], store
    )
    yield


def kernel(*refs):
    ending = []
    for _ in stages(*refs, ending):
        pass
    for wait in ending:
        wait()


def on_device(flow_state, mode_weight, bypass_weight, bias_term):
    hbm = pl.BlockSpec(memory_space=pltpu.HBM)
    pair = lambda *shape: [pltpu.VMEM(shape, BF)] * 2
    return pl.pallas_call(
        kernel,
        out_shape=jax.ShapeDtypeStruct(flow_state.shape, BF),
        in_specs=[hbm] * 5,
        out_specs=pl.BlockSpec(memory_space=pltpu.VMEM),
        scratch_shapes=[
            pltpu.VMEM(flow_state.shape, BF),
            pltpu.VMEM(mode_weight.shape, BF),
            pltpu.VMEM(bypass_weight.shape, BF),
            pltpu.VMEM((1, C), F32),
            pltpu.VMEM((ROWS, 256), BF),
            *pair(8, 2, 16, 256),
            *pair(4, 32, 2, 128),
            *pair(2, 32, 4, 128),
            pltpu.VMEM((2, 2, 8, 4, 128), BF),
            pltpu.VMEM((2, 32, 4, 128), BF),
            *pair(4, 32, 2, 128),
            *pair(8, 2, 2, 16, 128),
            pltpu.VMEM((2, 16, 32, 256), F32),
            pltpu.SemaphoreType.DMA((6,)),
            pltpu.SemaphoreType.DMA((6,)),
            pltpu.SemaphoreType.DMA,
            pltpu.SemaphoreType.DMA((8,)),
        ],
        compiler_params=pltpu.CompilerParams(
            collective_id=0, has_side_effects=True, vmem_limit_bytes=60 * 2**20
        ),
        name="fourier_layer",
    )(flow_state, mode_weight, bypass_weight, bias_term.reshape(1, C), tables())


def solution(mesh):
    in_specs = (P("row", "aisle", None, None), P(None, "row", "aisle", None, None), P(), P())
    return jax.shard_map(
        on_device,
        mesh=mesh,
        in_specs=in_specs,
        out_specs=P("row", "aisle", None, None),
        check_vma=False,
    )
```

```python
import math

import jax
import jax.numpy as jnp
import numpy as np
from jax import lax
from jax.experimental import pallas as pl
from jax.experimental.pallas import tpu as pltpu
from jax.sharding import PartitionSpec as P

C = 32
MX = 64
MY = 64
MZ = 32
NX = 64
NY = 256
NZ = 256
NR = 32
NA = 16
SCALING = 1.0 / math.sqrt(NX * NY * NZ)
BF = jnp.bfloat16
F32 = jnp.float32
MESH = pl.DeviceIdType.MESH


def twiddle(frequencies, positions, length):
    phase = np.mod(frequencies[:, None] * positions[None, :], length).astype(np.float32)
    angles = phase * np.float32(2.0 * math.pi / length)
    return np.cos(angles), np.sin(angles)


def tables():
    cz, sz = twiddle(np.arange(MZ), np.arange(NZ), NZ)
    weight = np.where(np.arange(MZ) == 0, 1.0, 2.0).astype(np.float32)[:, None]
    forward = np.stack([cz, -sz], 0)
    inverse = np.stack([weight * cz, -weight * sz], 0)
    fz = np.zeros((2, 2, NZ, 2, 2, 2, MZ), np.float32)
    iz = np.zeros((2, 2, 2, 2, 2, MZ, NZ), np.float32)
    for x in range(2):
        for c in range(2):
            fz[x, c, :, :, c, x, :] = forward.transpose(2, 0, 1)
            iz[x, c, :, c, x] = inverse
    fz = fz.reshape(4, 256, 256)
    iz = iz.reshape(4, 256, 256)
    eye = np.eye(16, dtype=np.float32)
    perm = np.einsum("ab,cd->acdb", eye, eye).reshape(256, 256)
    cy, sy = twiddle(np.arange(MY) - MY // 2, np.arange(NY), NY)
    ty = np.stack([np.stack([cy, sy]), np.stack([-sy, cy])])
    t1 = ty.reshape(2, 2, 32, 2, 2, 128).transpose(4, 3, 2, 0, 1, 5).reshape(256, 256)
    cx, sx = twiddle(np.arange(MX) - MX // 2, np.arange(NX), NX)
    tx = np.stack([np.stack([cx, sx]), np.stack([-sx, cx])])
    t2 = tx.reshape(2, 2, MX, 32, 2).transpose(2, 0, 4, 3, 1).reshape(128, 128)
    bx = np.stack([np.stack([cx, -sx]), np.stack([sx, cx])])
    t3 = bx.reshape(2, 2, MX, 32, 2).transpose(4, 3, 0, 2, 1).reshape(128, 128)
    by = np.stack([np.stack([cy, -sy]), np.stack([sy, cy])])
    t4 = by.reshape(2, 2, 32, 2, 2, 128).transpose(0, 5, 4, 3, 2, 1).reshape(256, 256)
    spread = np.einsum("ab,ij,cd,o->iacdbjo", np.eye(8), np.eye(2), np.eye(4), np.ones(32))
    spread = spread.reshape(64, 2048)
    fold = np.einsum("lm,ab,ij,cd,g->liacdgmbj", np.eye(2), np.eye(8), np.eye(2), np.eye(4), np.ones(4))
    fold = fold.reshape(128, 512)
    halves = lambda t: np.concatenate(np.split(t, t.shape[1] // 256, 1), 0)
    packed = [
        fz.reshape(1024, 256),
        perm,
        t1,
        np.concatenate([t2, t3], 1),
        halves(spread),
        halves(fold),
        t4,
        iz.reshape(1024, 256),
    ]
    return jnp.asarray(np.concatenate(packed, 0), BF)


FZ = 0
PERM = 1024
T1 = 1280
T23 = 1536
SPREAD = 1664
FOLD = 2176
T4 = 2432
IZ = 2688
ROWS = 3712
GROUPS = ((FZ, T1), (T1, SPREAD), (SPREAD, T4), (T4, ROWS))


def dot(left, right):
    return jnp.dot(left, right, preferred_element_type=F32)


def dot_tn(left, right):
    return lax.dot_general(left, right, (((0,), (0,)), ((), ())), preferred_element_type=F32)


def dot_nt(left, right):
    return lax.dot_general(left, right, (((1,), (1,)), ((), ())), preferred_element_type=F32)


def exchange_halves(first, second, roll):
    low = (lax.broadcasted_iota(jnp.int32, first.shape, 1) & 32) == 0
    return (
        jnp.where(low, first, roll(second, 32, 1)),
        jnp.where(low, roll(first, 96, 1), second),
    )


def stage_z(flow, fz, perm):
    total = None
    for x in range(2):
        for c in range(2):
            part = dot(flow[x, :, c * 16 : c * 16 + 16, :].reshape(256, 256), fz[2 * x + c])
            total = part if total is None else total + part
    return dot(perm, total.astype(BF)).astype(BF)


def near(place, index):
    return ((index - place + 10) & 7) < 4


def near_tables(place, t1, t4):
    columns = (lax.broadcasted_iota(jnp.int32, (128, 256), 1) >> 5) & 3
    rows = (lax.broadcasted_iota(jnp.int32, (256, 128), 0) >> 5) & 3
    first, second = t1[:128].astype(F32), t1[128:].astype(F32)
    left, right = t4[:, :128].astype(F32), t4[:, 128:].astype(F32)
    return (
        jnp.where(near(place, columns), first, second).astype(BF),
        jnp.where(near(place, rows), left, right).astype(BF),
    )


def stage_y(gathered, t1, roll):
    wide = jnp.concatenate(gathered, 1)
    upper = jnp.concatenate([wide[:, 0:128], wide[:, 256:384]], 1)
    lower = jnp.concatenate([wide[:, 128:256], wide[:, 384:512]], 1)
    sums = dot(t1, jnp.concatenate([upper, lower], 0))
    parts = [
        exchange_halves(sums[:64, c * 128 : c * 128 + 128], sums[64:, c * 128 : c * 128 + 128], roll)
        for c in range(2)
    ]
    return [parts[c][x] for x in range(2) for c in range(2)]


def stage_mix(modes, spread, fold, weight):
    planes = []
    for p in range(2):
        wide = dot_tn(modes, spread[:, p * 1024 : p * 1024 + 1024])
        real = [None, None]
        imag = [None, None]
        for q in range(2):
            for c in range(2):
                rows = slice(c * 64 + q * 32, c * 64 + q * 32 + 32)
                for h in range(4):
                    mr = wide[rows, h * 128 : h * 128 + 128]
                    mi = wide[rows, 512 + h * 128 : 512 + h * 128 + 128]
                    wr = weight(0, p, q, c * 512 + h * 128).astype(F32)
                    wi = weight(1, p, q, c * 512 + h * 128).astype(F32)
                    re = mr * wr - mi * wi
                    im = mr * wi + mi * wr
                    real[q] = re if real[q] is None else real[q] + re
                    imag[q] = im if imag[q] is None else imag[q] + im
        planes += [jnp.concatenate(real, 0), jnp.concatenate(imag, 0)]
    total = jnp.concatenate(planes, 1)
    high = total.astype(BF)
    low = (total - high.astype(F32)).astype(BF)
    mixed = dot_nt(fold, high) + dot_nt(fold, low)
    return jnp.concatenate([mixed[:64], mixed[64:]], 1)


def stage_y_back(parts, t4, roll):
    columns = []
    for o in range(2):
        low, high = exchange_halves(parts[o].astype(F32), parts[2 + o].astype(F32), roll)
        columns.append(jnp.concatenate([low, high], 0).astype(BF))
    return dot(t4, jnp.concatenate(columns, 1))


def bypass_matrix(bypass, lanes):
    wide = dot(bypass, lanes).astype(BF)
    tall = jnp.concatenate([wide] * 8, 0)
    rows = lax.broadcasted_iota(jnp.int32, (256, 256), 0) // 32
    columns = lax.broadcasted_iota(jnp.int32, (256, 256), 1) // 32
    return jnp.where(rows == columns, tall, jnp.zeros_like(tall))


def stage_z_back(planes, perm, iz, bypass, store):
    rows = dot(perm, planes).astype(BF)
    for x in range(2):
        for o in range(2):
            spectral = dot(rows, iz[2 * x + o]) * SCALING
            total = spectral.reshape(16, 16, 256) + bypass(x, o)
            store(x, o, jax.nn.gelu(total).astype(BF))


def stages(
    flow_hbm, weight_hbm, bypass_hbm, bias_hbm, table_hbm,
    out,
    flow, weight, bypass, bias, table,
    send_a, recv_a, send_b, recv_b, send_c, recv_c, send_d, recv_d, send_e, recv_e, send_f, recv_f,
    plain, send_sem, recv_sem, own_sem, load_sem, ending,
):
    row = lax.axis_index("row")
    aisle = lax.axis_index("aisle")
    held = (row - 2 * aisle + NR) % NR
    quad = held // 2
    half = row % 2
    place = aisle // 2
    side = aisle % 2
    group = aisle % 8

    loads = [pltpu.make_async_copy(flow_hbm, flow, load_sem.at[0])]
    for i, (first, last) in enumerate(GROUPS):
        part = pl.ds(first, last - first)
        loads.append(pltpu.make_async_copy(table_hbm.at[part], table.at[part], load_sem.at[i + 1]))
    loads.append(pltpu.make_async_copy(bypass_hbm, bypass, load_sem.at[5]))
    loads.append(pltpu.make_async_copy(bias_hbm, bias, load_sem.at[6]))
    loads.append(pltpu.make_async_copy(weight_hbm, weight, load_sem.at[7]))
    for load in loads:
        load.start()

    barrier = pltpu.get_barrier_semaphore()

    def away(i):
        return (12 + (i + 1) // 2 * (1 - 2 * (i % 2))) % 8

    def row_at(i):
        low = (row // 16 + 1 - i % 4 // 2) % 2
        return low * 16 + (row // 2 + away(i // 4)) % 8 * 2 + (row + 1 - i % 2) % 2

    def aisle_at(step, other):
        return (place + step + 8) % 8 * 2 + (side + other) % 2

    for step in (-3, -2, -1, 1, 0):
        for other in (1, 0):
            if step or other:
                to = aisle_at(step, other)
                pl.semaphore_signal(barrier, inc=1, device_id=(row, to), device_id_type=MESH)

    @pl.loop(0, NR - 1)
    def _(i):
        pl.semaphore_signal(barrier, inc=1, device_id=(row_at(i), aisle), device_id_type=MESH)

    def tile(first, rows=256):
        return table[first : first + rows]

    loads[0].wait()
    loads[1].wait()
    fz = [tile(FZ + 256 * i) for i in range(4)]
    send_a[...] = stage_z(flow, fz, tile(PERM)).reshape(8, 2, 16, 256)
    pl.semaphore_wait(barrier, 9 + NR - 1)

    def remote(stage, source, target, device):
        pltpu.make_async_remote_copy(
            src_ref=source,
            dst_ref=target,
            send_sem=send_sem.at[stage],
            recv_sem=recv_sem.at[stage],
            device_id=device,
            device_id_type=MESH,
        ).start()

    def local(stage, source, target):
        pltpu.make_async_copy(source, target, recv_sem.at[stage]).start()

    def arrived(stage, whole):
        pltpu.make_async_copy(whole, whole, recv_sem.at[stage]).wait()

    def sent(stage, part):
        pltpu.make_async_copy(part, part, send_sem.at[stage]).wait()

    for step in (2, -1, 1, 0):
        for other in (1, 0):
            to = aisle_at(step, other)
            if step or other:
                remote(0, send_a.at[to % 8], recv_a.at[group], (row, to))
    local(0, send_a.at[group], recv_a.at[group])

    ending.append(lambda: sent(0, send_a.at[pl.ds(0, 7)]))

    loads[5].wait()
    loads[6].wait()
    lanes = (
        lax.broadcasted_iota(jnp.int32, (32, 256), 0)
        == lax.broadcasted_iota(jnp.int32, (32, 256), 1) % 32
    ).astype(F32).astype(BF)
    diagonal = bypass_matrix(bypass[...], lanes)
    eye = lax.broadcasted_iota(jnp.int32, (32, 32), 0) == lax.broadcasted_iota(jnp.int32, (32, 32), 1)
    column = jnp.sum(jnp.where(eye, bias[...], 0.0), axis=1, keepdims=True)
    tall = jnp.concatenate([column] * 8, 0)
    for x in range(2):
        for y in range(2):
            field = flow[x, y * 8 : y * 8 + 8].reshape(256, 256)
            plain[x, y * 8 : y * 8 + 8] = (dot_tn(diagonal, field) + tall).reshape(8, 32, 256)

    for i in (2, 3, 4, 7):
        loads[i].wait()
    t1, t4 = near_tables(place, tile(T1), tile(T4))
    arrived(0, recv_a)
    yield
    parts = stage_y([recv_a[:, c].reshape(128, 256) for c in range(2)], t1, pltpu.roll)
    for i in range(4):
        send_b.reshape(256, 128)[i * 64 : i * 64 + 64] = parts[i].astype(BF)

    @pl.loop(0, NR - 1)
    def _(i):
        to = row_at(i)
        pair = (to - 2 * aisle + NR) % NR
        remote(1, send_b.at[:, pair], recv_b.at[:, row], (to, aisle))

    local(1, send_b.at[:, held], recv_b.at[:, row])

    ending.append(lambda: sent(1, send_b.at[:, pl.ds(0, NR - 1)]))
    arrived(1, recv_b)
    yield
    whole = recv_b.reshape(256, 128)[...]
    columns = [jnp.concatenate([whole[c * 64 : c * 64 + 64], whole[128 + c * 64 : 192 + c * 64]], 0) for c in range(2)]
    modes = (dot(tile(T23, 128)[:, :128], jnp.concatenate(columns, 1)) * SCALING).astype(BF)
    for c in range(2):
        send_c.reshape(256, 128)[c * 128 : c * 128 + 128] = modes[:, c * 128 : c * 128 + 128]

    mine = quad == aisle
    slot = half * 16 + aisle

    @pl.loop(0, NR - 1)
    def _(i):
        to = row_at(i)
        remote(2, send_c.at[:, to], recv_c.at[:, slot], (to, quad))

    @pl.when(mine)
    def _():
        local(2, send_c.at[:, row], recv_c.at[:, slot])

    @pl.when(jnp.logical_not(mine))
    def _():
        pltpu.make_async_remote_copy(
            src_ref=send_c.at[:, row],
            dst_ref=recv_c.at[:, slot],
            send_sem=own_sem,
            recv_sem=recv_sem.at[2],
            device_id=(row, quad),
            device_id_type=MESH,
        ).start()

    ending.append(lambda: sent(2, send_c.at[:, pl.ds(0, NR - 1)]))
    @ending.append
    def _():
        @pl.when(jnp.logical_not(mine))
        def _():
            pltpu.make_async_copy(send_c.at[:, 0], send_c.at[:, 0], own_sem).wait()

    arrived(2, recv_c)
    yield

    spread = jnp.concatenate([tile(SPREAD + 64 * i, 64) for i in range(8)], 1)
    fold = jnp.concatenate([tile(FOLD, 128), tile(FOLD + 128, 128)], 1)
    whole = recv_c.reshape(256, 128)[...]
    for h in range(2):
        modes = []
        for c in range(2):
            first = c * 128 + h * 64
            modes.append(whole[first : first + 32].astype(F32) + whole[first + 32 : first + 64].astype(F32))
        mixed = stage_mix(
            jnp.concatenate(modes, 0).astype(BF),
            spread,
            fold,
            lambda r, p, q, lane: weight[r, p, 2 * h + q, :, lane : lane + 128],
        )
        send_d.reshape(128, 128)[h * 64 : h * 64 + 64] = mixed.astype(BF)

    @pl.loop(0, 32)
    def _(i):
        h = i % 2
        to = (place + away(i // 4)) % 8 * 2 + (side + 1 - i % 4 // 2) % 2
        target_row = (aisle + to) % 16 * 2 + h
        same = jnp.logical_and(target_row == row, to == aisle)

        @pl.when(same)
        def _():
            local(3, send_d.at[h, :, to % 8], recv_d.at[:, row])

        @pl.when(jnp.logical_not(same))
        def _():
            remote(3, send_d.at[h, :, to % 8], recv_d.at[:, row], (target_row, to))

    @ending.append
    def _():
        @pl.when(mine)
        def _():
            sent(3, recv_d.at[:, pl.ds(0, 31)])

        @pl.when(jnp.logical_not(mine))
        def _():
            sent(3, recv_d)

    arrived(3, recv_d)
    yield
    whole = recv_d.reshape(256, 128)[...]
    back = dot(tile(T23, 128)[:, 128:], jnp.concatenate([whole[:128], whole[128:]], 1)).astype(BF)
    for x in range(2):
        for o in range(2):
            i = 2 * x + o
            send_e.reshape(256, 128)[i * 64 : i * 64 + 64] = back[x * 64 : x * 64 + 64, o * 128 : o * 128 + 128]

    @pl.loop(0, NR - 1)
    def _(i):
        to = row_at(i)
        remote(4, send_e.at[:, to], recv_e.at[:, held], (to, aisle))

    local(4, send_e.at[:, row], recv_e.at[:, held])

    ending.append(lambda: sent(4, send_e.at[:, pl.ds(0, NR - 1)]))
    arrived(4, recv_e)
    yield
    whole = recv_e.reshape(256, 128)[...]
    back = stage_y_back([whole[i * 64 : i * 64 + 64] for i in range(4)], t4, pltpu.roll).astype(BF)
    for r in range(2):
        for o in range(2):
            part = back[r * 128 : r * 128 + 128, o * 128 : o * 128 + 128]
            send_f[:, r, o] = part.reshape(8, 16, 128)

    for step in (-2, -1, 1, 0):
        for other in (1, 0):
            to = aisle_at(step, other)
            if step or other:
                remote(5, send_f.at[to % 8], recv_f.at[group], (row, to))
    local(5, send_f.at[group], recv_f.at[group])

    ending.append(lambda: sent(5, send_f.at[pl.ds(0, 7)]))
    arrived(5, recv_f)
    yield
    planes = jnp.concatenate(
        [recv_f[:, 0].reshape(256, 128), recv_f[:, 1].reshape(256, 128)], 1
    )

    iz = [tile(IZ + 256 * i) for i in range(4)]

    def store(x, o, value):
        out[x, :, o * 16 : o * 16 + 16, :] = value

    stage_z_back(
        planes, tile(PERM), iz, lambda x, o: plain[x, :, o * 16 : o * 16 + 16, :], store
    )
    yield


def kernel(*refs):
    ending = []
    for _ in stages(*refs, ending):
        pass
    for wait in ending:
        wait()


def on_device(flow_state, mode_weight, bypass_weight, bias_term):
    hbm = pl.BlockSpec(memory_space=pltpu.HBM)
    pair = lambda *shape: [pltpu.VMEM(shape, BF)] * 2
    return pl.pallas_call(
        kernel,
        out_shape=jax.ShapeDtypeStruct(flow_state.shape, BF),
        in_specs=[hbm] * 5,
        out_specs=pl.BlockSpec(memory_space=pltpu.VMEM),
        scratch_shapes=[
            pltpu.VMEM(flow_state.shape, BF),
            pltpu.VMEM(mode_weight.shape, BF),
            pltpu.VMEM(bypass_weight.shape, BF),
            pltpu.VMEM((1, C), F32),
            pltpu.VMEM((ROWS, 256), BF),
            *pair(8, 2, 16, 256),
            *pair(4, 32, 2, 128),
            *pair(2, 32, 4, 128),
            pltpu.VMEM((2, 2, 8, 4, 128), BF),
            pltpu.VMEM((2, 32, 4, 128), BF),
            *pair(4, 32, 2, 128),
            *pair(8, 2, 2, 16, 128),
            pltpu.VMEM((2, 16, 32, 256), F32),
            pltpu.SemaphoreType.DMA((6,)),
            pltpu.SemaphoreType.DMA((6,)),
            pltpu.SemaphoreType.DMA,
            pltpu.SemaphoreType.DMA((8,)),
        ],
        compiler_params=pltpu.CompilerParams(
            collective_id=0, has_side_effects=True, vmem_limit_bytes=60 * 2**20
        ),
        name="fourier_layer",
    )(flow_state, mode_weight, bypass_weight, bias_term.reshape(1, C), tables())


def solution(mesh):
    in_specs = (P("row", "aisle", None, None), P(None, "row", "aisle", None, None), P(), P())
    return jax.shard_map(
        on_device,
        mesh=mesh,
        in_specs=in_specs,
        out_specs=P("row", "aisle", None, None),
        check_vma=False,
    )
```

```python
import math

import jax
import jax.numpy as jnp
import numpy as np
from jax import lax
from jax.experimental import pallas as pl
from jax.experimental.pallas import tpu as pltpu
from jax.sharding import PartitionSpec as P

C = 32
MX = 64
MY = 64
MZ = 32
NX = 64
NY = 256
NZ = 256
NR = 32
NA = 16
SCALING = 1.0 / math.sqrt(NX * NY * NZ)
BF = jnp.bfloat16
F32 = jnp.float32
MESH = pl.DeviceIdType.MESH


def twiddle(frequencies, positions, length):
    phase = np.mod(frequencies[:, None] * positions[None, :], length).astype(np.float32)
    angles = phase * np.float32(2.0 * math.pi / length)
    return np.cos(angles), np.sin(angles)


def tables():
    cz, sz = twiddle(np.arange(MZ), np.arange(NZ), NZ)
    weight = np.where(np.arange(MZ) == 0, 1.0, 2.0).astype(np.float32)[:, None]
    forward = np.stack([cz, -sz], 0)
    inverse = np.stack([weight * cz, -weight * sz], 0)
    fz = np.zeros((2, 2, NZ, 2, 2, 2, MZ), np.float32)
    iz = np.zeros((2, 2, 2, 2, 2, MZ, NZ), np.float32)
    for x in range(2):
        for c in range(2):
            fz[x, c, :, :, c, x, :] = forward.transpose(2, 0, 1)
            iz[x, c, :, c, x] = inverse
    fz = fz.reshape(4, 256, 256)
    iz = iz.reshape(4, 256, 256)
    eye = np.eye(16, dtype=np.float32)
    perm = np.einsum("ab,cd->acdb", eye, eye).reshape(256, 256)
    cy, sy = twiddle(np.arange(MY) - MY // 2, np.arange(NY), NY)
    ty = np.stack([np.stack([cy, sy]), np.stack([-sy, cy])])
    t1 = ty.reshape(2, 2, 32, 2, 2, 128).transpose(4, 3, 2, 0, 1, 5).reshape(256, 256)
    cx, sx = twiddle(np.arange(MX) - MX // 2, np.arange(NX), NX)
    tx = np.stack([np.stack([cx, sx]), np.stack([-sx, cx])])
    t2 = tx.reshape(2, 2, MX, 32, 2).transpose(2, 0, 4, 3, 1).reshape(128, 128)
    bx = np.stack([np.stack([cx, -sx]), np.stack([sx, cx])])
    t3 = bx.reshape(2, 2, MX, 32, 2).transpose(4, 3, 0, 2, 1).reshape(128, 128)
    by = np.stack([np.stack([cy, -sy]), np.stack([sy, cy])])
    t4 = by.reshape(2, 2, 32, 2, 2, 128).transpose(0, 5, 4, 3, 2, 1).reshape(256, 256)
    spread = np.einsum("ab,ij,cd,o->iacdbjo", np.eye(8), np.eye(2), np.eye(4), np.ones(32))
    spread = spread.reshape(64, 2048)
    fold = np.einsum("lm,ab,ij,cd,g->liacdgmbj", np.eye(2), np.eye(8), np.eye(2), np.eye(4), np.ones(4))
    fold = fold.reshape(128, 512)
    halves = lambda t: np.concatenate(np.split(t, t.shape[1] // 256, 1), 0)
    packed = [
        fz.reshape(1024, 256),
        perm,
        t1,
        np.concatenate([t2, t3], 1),
        halves(spread),
        halves(fold),
        t4,
        iz.reshape(1024, 256),
    ]
    return jnp.asarray(np.concatenate(packed, 0), BF)


FZ = 0
PERM = 1024
T1 = 1280
T23 = 1536
SPREAD = 1664
FOLD = 2176
T4 = 2432
IZ = 2688
ROWS = 3712
GROUPS = ((FZ, T1), (T1, SPREAD), (SPREAD, T4), (T4, ROWS))


def dot(left, right):
    return jnp.dot(left, right, preferred_element_type=F32)


def dot_tn(left, right):
    return lax.dot_general(left, right, (((0,), (0,)), ((), ())), preferred_element_type=F32)


def dot_nt(left, right):
    return lax.dot_general(left, right, (((1,), (1,)), ((), ())), preferred_element_type=F32)


def exchange_halves(first, second, roll):
    low = (lax.broadcasted_iota(jnp.int32, first.shape, 1) & 32) == 0
    return (
        jnp.where(low, first, roll(second, 32, 1)),
        jnp.where(low, roll(first, 96, 1), second),
    )


def stage_z(flow, fz, perm):
    total = None
    for x in range(2):
        for c in range(2):
            part = dot(flow[x, :, c * 16 : c * 16 + 16, :].reshape(256, 256), fz[2 * x + c])
            total = part if total is None else total + part
    return dot(perm, total.astype(BF)).astype(BF)


def near(place, index):
    return ((index - place + 10) & 7) < 4


def near_tables(place, t1, t4):
    columns = (lax.broadcasted_iota(jnp.int32, (128, 256), 1) >> 5) & 3
    rows = (lax.broadcasted_iota(jnp.int32, (256, 128), 0) >> 5) & 3
    first, second = t1[:128].astype(F32), t1[128:].astype(F32)
    left, right = t4[:, :128].astype(F32), t4[:, 128:].astype(F32)
    return (
        jnp.where(near(place, columns), first, second).astype(BF),
        jnp.where(near(place, rows), left, right).astype(BF),
    )


def stage_y(gathered, t1, roll):
    wide = jnp.concatenate(gathered, 1)
    upper = jnp.concatenate([wide[:, 0:128], wide[:, 256:384]], 1)
    lower = jnp.concatenate([wide[:, 128:256], wide[:, 384:512]], 1)
    sums = dot(t1, jnp.concatenate([upper, lower], 0))
    parts = [
        exchange_halves(sums[:64, c * 128 : c * 128 + 128], sums[64:, c * 128 : c * 128 + 128], roll)
        for c in range(2)
    ]
    return [parts[c][x] for x in range(2) for c in range(2)]


def stage_mix(modes, spread, fold, weight):
    planes = []
    for p in range(2):
        wide = dot_tn(modes, spread[:, p * 1024 : p * 1024 + 1024])
        real = [None, None]
        imag = [None, None]
        for q in range(2):
            for c in range(2):
                rows = slice(c * 64 + q * 32, c * 64 + q * 32 + 32)
                for h in range(4):
                    mr = wide[rows, h * 128 : h * 128 + 128]
                    mi = wide[rows, 512 + h * 128 : 512 + h * 128 + 128]
                    wr = weight(0, p, q, c * 512 + h * 128).astype(F32)
                    wi = weight(1, p, q, c * 512 + h * 128).astype(F32)
                    re = mr * wr - mi * wi
                    im = mr * wi + mi * wr
                    real[q] = re if real[q] is None else real[q] + re
                    imag[q] = im if imag[q] is None else imag[q] + im
        planes += [jnp.concatenate(real, 0), jnp.concatenate(imag, 0)]
    total = jnp.concatenate(planes, 1)
    high = total.astype(BF)
    low = (total - high.astype(F32)).astype(BF)
    mixed = dot_nt(fold, high) + dot_nt(fold, low)
    return jnp.concatenate([mixed[:64], mixed[64:]], 1)


def stage_y_back(parts, t4, roll):
    columns = []
    for o in range(2):
        low, high = exchange_halves(parts[o].astype(F32), parts[2 + o].astype(F32), roll)
        columns.append(jnp.concatenate([low, high], 0).astype(BF))
    return dot(t4, jnp.concatenate(columns, 1))


def bypass_matrix(bypass, lanes):
    wide = dot(bypass, lanes).astype(BF)
    tall = jnp.concatenate([wide] * 8, 0)
    rows = lax.broadcasted_iota(jnp.int32, (256, 256), 0) // 32
    columns = lax.broadcasted_iota(jnp.int32, (256, 256), 1) // 32
    return jnp.where(rows == columns, tall, jnp.zeros_like(tall))


def stage_z_back(planes, perm, iz, bypass, store):
    rows = dot(perm, planes).astype(BF)
    for x in range(2):
        for o in range(2):
            spectral = dot(rows, iz[2 * x + o]) * SCALING
            total = spectral.reshape(16, 16, 256) + bypass(x, o)
            store(x, o, jax.nn.gelu(total).astype(BF))


def stages(
    flow_hbm, weight_hbm, bypass_hbm, bias_hbm, table_hbm,
    out,
    flow, weight, bypass, bias, table,
    send_a, recv_a, send_b, recv_b, send_c, recv_c, send_d, recv_d, send_e, recv_e, send_f, recv_f,
    plain, send_sem, recv_sem, own_sem, load_sem, ending,
):
    row = lax.axis_index("row")
    aisle = lax.axis_index("aisle")
    held = (row - 2 * aisle + NR) % NR
    quad = held // 2
    half = row % 2
    place = aisle // 2
    side = aisle % 2
    group = aisle % 8

    loads = [pltpu.make_async_copy(flow_hbm, flow, load_sem.at[0])]
    for i, (first, last) in enumerate(GROUPS):
        part = pl.ds(first, last - first)
        loads.append(pltpu.make_async_copy(table_hbm.at[part], table.at[part], load_sem.at[i + 1]))
    loads.append(pltpu.make_async_copy(bypass_hbm, bypass, load_sem.at[5]))
    loads.append(pltpu.make_async_copy(bias_hbm, bias, load_sem.at[6]))
    loads.append(pltpu.make_async_copy(weight_hbm, weight, load_sem.at[7]))
    for load in loads:
        load.start()

    barrier = pltpu.get_barrier_semaphore()

    def away(i):
        return (12 + (i + 1) // 2 * (1 - 2 * (i % 2))) % 8

    def row_at(i):
        low = (row // 16 + 1 - i % 4 // 2) % 2
        return low * 16 + (row // 2 + away(i // 4)) % 8 * 2 + (row + 1 - i % 2) % 2

    def aisle_at(step, other):
        return (place + step + 8) % 8 * 2 + (side + other) % 2

    for step in (-3, -2, -1, 1, 0):
        for other in (1, 0):
            if step or other:
                to = aisle_at(step, other)
                pl.semaphore_signal(barrier, inc=1, device_id=(row, to), device_id_type=MESH)

    @pl.loop(0, NR - 1)
    def _(i):
        pl.semaphore_signal(barrier, inc=1, device_id=(row_at(i), aisle), device_id_type=MESH)

    def tile(first, rows=256):
        return table[first : first + rows]

    loads[0].wait()
    loads[1].wait()
    fz = [tile(FZ + 256 * i) for i in range(4)]
    send_a[...] = stage_z(flow, fz, tile(PERM)).reshape(8, 2, 16, 256)
    pl.semaphore_wait(barrier, 9 + NR - 1)

    def remote(stage, source, target, device):
        pltpu.make_async_remote_copy(
            src_ref=source,
            dst_ref=target,
            send_sem=send_sem.at[stage],
            recv_sem=recv_sem.at[stage],
            device_id=device,
            device_id_type=MESH,
        ).start()

    def local(stage, source, target):
        pltpu.make_async_copy(source, target, recv_sem.at[stage]).start()

    def arrived(stage, whole):
        pltpu.make_async_copy(whole, whole, recv_sem.at[stage]).wait()

    def sent(stage, part):
        pltpu.make_async_copy(part, part, send_sem.at[stage]).wait()

    for step in (2, -1, 1, 0):
        for other in (1, 0):
            to = aisle_at(step, other)
            if step or other:
                remote(0, send_a.at[to % 8], recv_a.at[group], (row, to))
    local(0, send_a.at[group], recv_a.at[group])

    ending.append(lambda: sent(0, send_a.at[pl.ds(0, 7)]))

    loads[5].wait()
    loads[6].wait()
    lanes = (
        lax.broadcasted_iota(jnp.int32, (32, 256), 0)
        == lax.broadcasted_iota(jnp.int32, (32, 256), 1) % 32
    ).astype(F32).astype(BF)
    diagonal = bypass_matrix(bypass[...], lanes)
    eye = lax.broadcasted_iota(jnp.int32, (32, 32), 0) == lax.broadcasted_iota(jnp.int32, (32, 32), 1)
    column = jnp.sum(jnp.where(eye, bias[...], 0.0), axis=1, keepdims=True)
    tall = jnp.concatenate([column] * 8, 0)
    for x in range(2):
        for y in range(2):
            field = flow[x, y * 8 : y * 8 + 8].reshape(256, 256)
            plain[x, y * 8 : y * 8 + 8] = (dot_tn(diagonal, field) + tall).reshape(8, 32, 256)

    for i in (2, 3, 4, 7):
        loads[i].wait()
    t1, t4 = near_tables(place, tile(T1), tile(T4))
    arrived(0, recv_a)
    yield
    parts = stage_y([recv_a[:, c].reshape(128, 256) for c in range(2)], t1, pltpu.roll)
    for i in range(4):
        send_b.reshape(256, 128)[i * 64 : i * 64 + 64] = parts[i].astype(BF)

    @pl.loop(0, NR - 1)
    def _(i):
        to = row_at(i)
        pair = (to - 2 * aisle + NR) % NR
        remote(1, send_b.at[:, pair], recv_b.at[:, row], (to, aisle))

    local(1, send_b.at[:, held], recv_b.at[:, row])

    ending.append(lambda: sent(1, send_b.at[:, pl.ds(0, NR - 1)]))
    arrived(1, recv_b)
    yield
    whole = recv_b.reshape(256, 128)[...]
    columns = [jnp.concatenate([whole[c * 64 : c * 64 + 64], whole[128 + c * 64 : 192 + c * 64]], 0) for c in range(2)]
    modes = (dot(tile(T23, 128)[:, :128], jnp.concatenate(columns, 1)) * SCALING).astype(BF)
    for c in range(2):
        send_c.reshape(256, 128)[c * 128 : c * 128 + 128] = modes[:, c * 128 : c * 128 + 128]

    mine = quad == aisle
    slot = half * 16 + aisle

    @pl.loop(0, NR - 1)
    def _(i):
        to = row_at(i)
        remote(2, send_c.at[:, to], recv_c.at[:, slot], (to, quad))

    @pl.when(mine)
    def _():
        local(2, send_c.at[:, row], recv_c.at[:, slot])

    @pl.when(jnp.logical_not(mine))
    def _():
        pltpu.make_async_remote_copy(
            src_ref=send_c.at[:, row],
            dst_ref=recv_c.at[:, slot],
            send_sem=own_sem,
            recv_sem=recv_sem.at[2],
            device_id=(row, quad),
            device_id_type=MESH,
        ).start()

    ending.append(lambda: sent(2, send_c.at[:, pl.ds(0, NR - 1)]))
    @ending.append
    def _():
        @pl.when(jnp.logical_not(mine))
        def _():
            pltpu.make_async_copy(send_c.at[:, 0], send_c.at[:, 0], own_sem).wait()

    arrived(2, recv_c)
    yield

    spread = jnp.concatenate([tile(SPREAD + 64 * i, 64) for i in range(8)], 1)
    fold = jnp.concatenate([tile(FOLD, 128), tile(FOLD + 128, 128)], 1)
    whole = recv_c.reshape(256, 128)[...]
    for h in range(2):
        modes = []
        for c in range(2):
            first = c * 128 + h * 64
            modes.append(whole[first : first + 32].astype(F32) + whole[first + 32 : first + 64].astype(F32))
        mixed = stage_mix(
            jnp.concatenate(modes, 0).astype(BF),
            spread,
            fold,
            lambda r, p, q, lane: weight[r, p, 2 * h + q, :, lane : lane + 128],
        )
        send_d.reshape(128, 128)[h * 64 : h * 64 + 64] = mixed.astype(BF)

    @pl.loop(0, 32)
    def _(i):
        h = i % 2
        to = (place + away(i // 4)) % 8 * 2 + (side + 1 - i % 4 // 2) % 2
        target_row = (aisle + to) % 16 * 2 + h
        same = jnp.logical_and(target_row == row, to == aisle)

        @pl.when(same)
        def _():
            local(3, send_d.at[h, :, to % 8], recv_d.at[:, row])

        @pl.when(jnp.logical_not(same))
        def _():
            remote(3, send_d.at[h, :, to % 8], recv_d.at[:, row], (target_row, to))

    @ending.append
    def _():
        @pl.when(mine)
        def _():
            sent(3, recv_d.at[:, pl.ds(0, 31)])

        @pl.when(jnp.logical_not(mine))
        def _():
            sent(3, recv_d)

    arrived(3, recv_d)
    yield
    whole = recv_d.reshape(256, 128)[...]
    back = dot(tile(T23, 128)[:, 128:], jnp.concatenate([whole[:128], whole[128:]], 1)).astype(BF)
    for x in range(2):
        for o in range(2):
            i = 2 * x + o
            send_e.reshape(256, 128)[i * 64 : i * 64 + 64] = back[x * 64 : x * 64 + 64, o * 128 : o * 128 + 128]

    @pl.loop(0, NR - 1)
    def _(i):
        to = row_at(i)
        remote(4, send_e.at[:, to], recv_e.at[:, held], (to, aisle))

    local(4, send_e.at[:, row], recv_e.at[:, held])

    ending.append(lambda: sent(4, send_e.at[:, pl.ds(0, NR - 1)]))
    arrived(4, recv_e)
    yield
    whole = recv_e.reshape(256, 128)[...]
    back = stage_y_back([whole[i * 64 : i * 64 + 64] for i in range(4)], t4, pltpu.roll).astype(BF)
    for r in range(2):
        for o in range(2):
            part = back[r * 128 : r * 128 + 128, o * 128 : o * 128 + 128]
            send_f[:, r, o] = part.reshape(8, 16, 128)

    for step in (-2, -1, 1, 0):
        for other in (1, 0):
            to = aisle_at(step, other)
            if step or other:
                remote(5, send_f.at[to % 8], recv_f.at[group], (row, to))
    local(5, send_f.at[group], recv_f.at[group])

    ending.append(lambda: sent(5, send_f.at[pl.ds(0, 7)]))
    arrived(5, recv_f)
    yield
    planes = jnp.concatenate(
        [recv_f[:, 0].reshape(256, 128), recv_f[:, 1].reshape(256, 128)], 1
    )

    iz = [tile(IZ + 256 * i) for i in range(4)]

    def store(x, o, value):
        out[x, :, o * 16 : o * 16 + 16, :] = value

    stage_z_back(
        planes, tile(PERM), iz, lambda x, o: plain[x, :, o * 16 : o * 16 + 16, :], store
    )
    yield


def kernel(*refs):
    ending = []
    for _ in stages(*refs, ending):
        pass
    for wait in ending:
        wait()


def on_device(flow_state, mode_weight, bypass_weight, bias_term):
    hbm = pl.BlockSpec(memory_space=pltpu.HBM)
    pair = lambda *shape: [pltpu.VMEM(shape, BF)] * 2
    return pl.pallas_call(
        kernel,
        out_shape=pltpu.VMEM(flow_state.shape, BF),
        in_specs=[hbm] * 5,
        out_specs=pl.BlockSpec(memory_space=pltpu.VMEM),
        scratch_shapes=[
            pltpu.VMEM(flow_state.shape, BF),
            pltpu.VMEM(mode_weight.shape, BF),
            pltpu.VMEM(bypass_weight.shape, BF),
            pltpu.VMEM((1, C), F32),
            pltpu.VMEM((ROWS, 256), BF),
            *pair(8, 2, 16, 256),
            *pair(4, 32, 2, 128),
            *pair(2, 32, 4, 128),
            pltpu.VMEM((2, 2, 8, 4, 128), BF),
            pltpu.VMEM((2, 32, 4, 128), BF),
            *pair(4, 32, 2, 128),
            *pair(8, 2, 2, 16, 128),
            pltpu.VMEM((2, 16, 32, 256), F32),
            pltpu.SemaphoreType.DMA((6,)),
            pltpu.SemaphoreType.DMA((6,)),
            pltpu.SemaphoreType.DMA,
            pltpu.SemaphoreType.DMA((8,)),
        ],
        compiler_params=pltpu.CompilerParams(
            collective_id=0, has_side_effects=True, vmem_limit_bytes=60 * 2**20
        ),
        name="fourier_layer",
    )(flow_state, mode_weight, bypass_weight, bias_term.reshape(1, C), tables())


def solution(mesh):
    in_specs = (P("row", "aisle", None, None), P(None, "row", "aisle", None, None), P(), P())
    return jax.shard_map(
        on_device,
        mesh=mesh,
        in_specs=in_specs,
        out_specs=P("row", "aisle", None, None),
        check_vma=False,
    )
```

```python
import math

import jax
import jax.numpy as jnp
import numpy as np
from jax import lax
from jax.experimental import pallas as pl
from jax.experimental.pallas import tpu as pltpu
from jax.sharding import PartitionSpec as P

C = 32
MX = 64
MY = 64
MZ = 32
NX = 64
NY = 256
NZ = 256
NR = 32
NA = 16
SCALING = 1.0 / math.sqrt(NX * NY * NZ)
BF = jnp.bfloat16
F32 = jnp.float32
MESH = pl.DeviceIdType.MESH


def twiddle(frequencies, positions, length):
    phase = np.mod(frequencies[:, None] * positions[None, :], length).astype(np.float32)
    angles = phase * np.float32(2.0 * math.pi / length)
    return np.cos(angles), np.sin(angles)


def tables():
    cz, sz = twiddle(np.arange(MZ), np.arange(NZ), NZ)
    weight = np.where(np.arange(MZ) == 0, 1.0, 2.0).astype(np.float32)[:, None]
    forward = np.stack([cz, -sz], 0)
    inverse = np.stack([weight * cz, -weight * sz], 0)
    fz = np.zeros((2, 2, NZ, 2, 2, 2, MZ), np.float32)
    iz = np.zeros((2, 2, 2, 2, 2, MZ, NZ), np.float32)
    for x in range(2):
        for c in range(2):
            fz[x, c, :, :, c, x, :] = forward.transpose(2, 0, 1)
            iz[x, c, :, c, x] = inverse
    fz = fz.reshape(4, 256, 256)
    iz = iz.reshape(4, 256, 256)
    eye = np.eye(16, dtype=np.float32)
    perm = np.einsum("ab,cd->acdb", eye, eye).reshape(256, 256)
    cy, sy = twiddle(np.arange(MY) - MY // 2, np.arange(NY), NY)
    ty = np.stack([np.stack([cy, sy]), np.stack([-sy, cy])])
    t1 = ty.reshape(2, 2, 32, 2, 2, 128).transpose(4, 3, 2, 0, 1, 5).reshape(256, 256)
    cx, sx = twiddle(np.arange(MX) - MX // 2, np.arange(NX), NX)
    tx = np.stack([np.stack([cx, sx]), np.stack([-sx, cx])])
    t2 = tx.reshape(2, 2, MX, 32, 2).transpose(2, 0, 4, 3, 1).reshape(128, 128)
    bx = np.stack([np.stack([cx, -sx]), np.stack([sx, cx])])
    t3 = bx.reshape(2, 2, MX, 32, 2).transpose(4, 3, 0, 2, 1).reshape(128, 128)
    by = np.stack([np.stack([cy, -sy]), np.stack([sy, cy])])
    t4 = by.reshape(2, 2, 32, 2, 2, 128).transpose(0, 5, 4, 3, 2, 1).reshape(256, 256)
    spread = np.einsum("ab,ij,cd,o->iacdbjo", np.eye(8), np.eye(2), np.eye(4), np.ones(32))
    spread = spread.reshape(64, 2048)
    fold = np.einsum("lm,ab,ij,cd,g->liacdgmbj", np.eye(2), np.eye(8), np.eye(2), np.eye(4), np.ones(4))
    fold = fold.reshape(128, 512)
    halves = lambda t: np.concatenate(np.split(t, t.shape[1] // 256, 1), 0)
    packed = [
        fz.reshape(1024, 256),
        perm,
        t1,
        np.concatenate([t2, t3], 1),
        halves(spread),
        halves(fold),
        t4,
        iz.reshape(1024, 256),
    ]
    return jnp.asarray(np.concatenate(packed, 0), BF)


FZ = 0
PERM = 1024
T1 = 1280
T23 = 1536
SPREAD = 1664
FOLD = 2176
T4 = 2432
IZ = 2688
ROWS = 3712
GROUPS = ((FZ, T1), (T1, SPREAD), (SPREAD, T4), (T4, ROWS))


def dot(left, right):
    return jnp.dot(left, right, preferred_element_type=F32)


def dot_tn(left, right):
    return lax.dot_general(left, right, (((0,), (0,)), ((), ())), preferred_element_type=F32)


def dot_nt(left, right):
    return lax.dot_general(left, right, (((1,), (1,)), ((), ())), preferred_element_type=F32)


def exchange_halves(first, second, roll):
    low = (lax.broadcasted_iota(jnp.int32, first.shape, 1) & 32) == 0
    return (
        jnp.where(low, first, roll(second, 32, 1)),
        jnp.where(low, roll(first, 96, 1), second),
    )


def stage_z(flow, fz, perm):
    total = None
    for x in range(2):
        for c in range(2):
            part = dot(flow[x, :, c * 16 : c * 16 + 16, :].reshape(256, 256), fz[2 * x + c])
            total = part if total is None else total + part
    return dot(perm, total.astype(BF)).astype(BF)


def near(place, index):
    return ((index - place + 10) & 7) < 4


def near_tables(place, t1, t4):
    columns = (lax.broadcasted_iota(jnp.int32, (128, 256), 1) >> 5) & 3
    rows = (lax.broadcasted_iota(jnp.int32, (256, 128), 0) >> 5) & 3
    first, second = t1[:128].astype(F32), t1[128:].astype(F32)
    left, right = t4[:, :128].astype(F32), t4[:, 128:].astype(F32)
    return (
        jnp.where(near(place, columns), first, second).astype(BF),
        jnp.where(near(place, rows), left, right).astype(BF),
    )


def stage_y(gathered, t1, roll):
    wide = jnp.concatenate(gathered, 1)
    upper = jnp.concatenate([wide[:, 0:128], wide[:, 256:384]], 1)
    lower = jnp.concatenate([wide[:, 128:256], wide[:, 384:512]], 1)
    sums = dot(t1, jnp.concatenate([upper, lower], 0))
    parts = [
        exchange_halves(sums[:64, c * 128 : c * 128 + 128], sums[64:, c * 128 : c * 128 + 128], roll)
        for c in range(2)
    ]
    return [parts[c][x] for x in range(2) for c in range(2)]


def stage_mix(modes, spread, fold, weight):
    planes = []
    for p in range(2):
        wide = dot_tn(modes, spread[:, p * 1024 : p * 1024 + 1024])
        real = [None, None]
        imag = [None, None]
        for q in range(2):
            for c in range(2):
                rows = slice(c * 64 + q * 32, c * 64 + q * 32 + 32)
                for h in range(4):
                    mr = wide[rows, h * 128 : h * 128 + 128]
                    mi = wide[rows, 512 + h * 128 : 512 + h * 128 + 128]
                    wr = weight(0, p, q, c * 512 + h * 128).astype(F32)
                    wi = weight(1, p, q, c * 512 + h * 128).astype(F32)
                    re = mr * wr - mi * wi
                    im = mr * wi + mi * wr
                    real[q] = re if real[q] is None else real[q] + re
                    imag[q] = im if imag[q] is None else imag[q] + im
        planes += [jnp.concatenate(real, 0), jnp.concatenate(imag, 0)]
    total = jnp.concatenate(planes, 1)
    mixed = dot_nt(fold, total.astype(BF))
    return jnp.concatenate([mixed[:64], mixed[64:]], 1)


def stage_y_back(parts, t4, roll):
    columns = []
    for o in range(2):
        low, high = exchange_halves(parts[o].astype(F32), parts[2 + o].astype(F32), roll)
        columns.append(jnp.concatenate([low, high], 0).astype(BF))
    return dot(t4, jnp.concatenate(columns, 1))


def bypass_matrix(bypass, lanes):
    wide = dot(bypass, lanes).astype(BF)
    tall = jnp.concatenate([wide] * 8, 0)
    rows = lax.broadcasted_iota(jnp.int32, (256, 256), 0) // 32
    columns = lax.broadcasted_iota(jnp.int32, (256, 256), 1) // 32
    return jnp.where(rows == columns, tall, jnp.zeros_like(tall))


def stage_z_back(planes, perm, iz, bypass, store):
    rows = dot(perm, planes).astype(BF)
    for x in range(2):
        for o in range(2):
            spectral = dot(rows, iz[2 * x + o]) * SCALING
            total = spectral.reshape(16, 16, 256) + bypass(x, o)
            store(x, o, jax.nn.gelu(total).astype(BF))


def stages(
    flow_hbm, weight_hbm, bypass_hbm, bias_hbm, table_hbm,
    out,
    flow, weight, bypass, bias, table,
    send_a, recv_a, send_b, recv_b, send_c, recv_c, send_d, recv_d, send_e, recv_e, send_f, recv_f,
    plain, send_sem, recv_sem, own_sem, load_sem, ending,
):
    row = lax.axis_index("row")
    aisle = lax.axis_index("aisle")
    held = (row - 2 * aisle) & (NR - 1)
    quad = held >> 1
    half = row & 1
    place = aisle >> 1
    side = aisle & 1
    group = aisle & 7

    loads = [pltpu.make_async_copy(flow_hbm, flow, load_sem.at[0])]
    for i, (first, last) in enumerate(GROUPS):
        part = pl.ds(first, last - first)
        loads.append(pltpu.make_async_copy(table_hbm.at[part], table.at[part], load_sem.at[i + 1]))
    loads.append(pltpu.make_async_copy(bypass_hbm, bypass, load_sem.at[5]))
    loads.append(pltpu.make_async_copy(bias_hbm, bias, load_sem.at[6]))
    loads.append(pltpu.make_async_copy(weight_hbm, weight, load_sem.at[7]))
    for load in loads:
        load.start()

    barrier = pltpu.get_barrier_semaphore()

    def away(i):
        return (12 + ((i + 1) >> 1) * (1 - 2 * (i & 1))) & 7

    def row_at(i):
        low = ((row >> 4) + 1 + (i >> 1)) & 1
        return low * 16 + (((row >> 1) + away(i >> 2)) & 7) * 2 + ((row + 1 + i) & 1)

    def aisle_at(step, other):
        return ((place + step) & 7) * 2 + ((side + other) & 1)

    for step in (-3, -2, -1, 1, 0):
        for other in (1, 0):
            if step or other:
                to = aisle_at(step, other)
                pl.semaphore_signal(barrier, inc=1, device_id=(row, to), device_id_type=MESH)

    @pl.loop(0, NR - 1)
    def _(i):
        pl.semaphore_signal(barrier, inc=1, device_id=(row_at(i), aisle), device_id_type=MESH)

    def tile(first, rows=256):
        return table[first : first + rows]

    loads[0].wait()
    loads[1].wait()
    fz = [tile(FZ + 256 * i) for i in range(4)]
    send_a[...] = stage_z(flow, fz, tile(PERM)).reshape(8, 2, 16, 256)
    pl.semaphore_wait(barrier, 9 + NR - 1)

    def remote(stage, source, target, device):
        pltpu.make_async_remote_copy(
            src_ref=source,
            dst_ref=target,
            send_sem=send_sem.at[stage],
            recv_sem=recv_sem.at[stage],
            device_id=device,
            device_id_type=MESH,
        ).start()

    def local(stage, source, target):
        pltpu.make_async_copy(source, target, recv_sem.at[stage]).start()

    def arrived(stage, whole):
        pltpu.make_async_copy(whole, whole, recv_sem.at[stage]).wait()

    def sent(stage, part):
        pltpu.make_async_copy(part, part, send_sem.at[stage]).wait()

    for step in (2, -1, 1, 0):
        for other in (1, 0):
            to = aisle_at(step, other)
            if step or other:
                remote(0, send_a.at[to & 7], recv_a.at[group], (row, to))
    local(0, send_a.at[group], recv_a.at[group])

    ending.append(lambda: sent(0, send_a.at[pl.ds(0, 7)]))

    loads[5].wait()
    loads[6].wait()
    lanes = (
        lax.broadcasted_iota(jnp.int32, (32, 256), 0)
        == lax.broadcasted_iota(jnp.int32, (32, 256), 1) % 32
    ).astype(F32).astype(BF)
    diagonal = bypass_matrix(bypass[...], lanes)
    eye = lax.broadcasted_iota(jnp.int32, (32, 32), 0) == lax.broadcasted_iota(jnp.int32, (32, 32), 1)
    column = jnp.sum(jnp.where(eye, bias[...], 0.0), axis=1, keepdims=True)
    tall = jnp.concatenate([column] * 8, 0)
    for x in range(2):
        for y in range(2):
            field = flow[x, y * 8 : y * 8 + 8].reshape(256, 256)
            plain[x, y * 8 : y * 8 + 8] = (dot_tn(diagonal, field) + tall).reshape(8, 32, 256)

    for i in (2, 3, 4, 7):
        loads[i].wait()
    t1, t4 = near_tables(place, tile(T1), tile(T4))
    arrived(0, recv_a)
    yield
    parts = stage_y([recv_a[:, c].reshape(128, 256) for c in range(2)], t1, pltpu.roll)
    for i in range(4):
        send_b.reshape(256, 128)[i * 64 : i * 64 + 64] = parts[i].astype(BF)

    @pl.loop(0, NR - 1)
    def _(i):
        to = row_at(i)
        pair = (to - 2 * aisle) & (NR - 1)
        remote(1, send_b.at[:, pair], recv_b.at[:, row], (to, aisle))

    local(1, send_b.at[:, held], recv_b.at[:, row])

    ending.append(lambda: sent(1, send_b.at[:, pl.ds(0, NR - 1)]))
    arrived(1, recv_b)
    yield
    whole = recv_b.reshape(256, 128)[...]
    columns = [jnp.concatenate([whole[c * 64 : c * 64 + 64], whole[128 + c * 64 : 192 + c * 64]], 0) for c in range(2)]
    modes = (dot(tile(T23, 128)[:, :128], jnp.concatenate(columns, 1)) * SCALING).astype(BF)
    for c in range(2):
        send_c.reshape(256, 128)[c * 128 : c * 128 + 128] = modes[:, c * 128 : c * 128 + 128]

    mine = quad == aisle
    slot = half * 16 + aisle

    @pl.loop(0, NR - 1)
    def _(i):
        to = row_at(i)
        remote(2, send_c.at[:, to], recv_c.at[:, slot], (to, quad))

    @pl.when(mine)
    def _():
        local(2, send_c.at[:, row], recv_c.at[:, slot])

    @pl.when(jnp.logical_not(mine))
    def _():
        pltpu.make_async_remote_copy(
            src_ref=send_c.at[:, row],
            dst_ref=recv_c.at[:, slot],
            send_sem=own_sem,
            recv_sem=recv_sem.at[2],
            device_id=(row, quad),
            device_id_type=MESH,
        ).start()

    ending.append(lambda: sent(2, send_c.at[:, pl.ds(0, NR - 1)]))
    @ending.append
    def _():
        @pl.when(jnp.logical_not(mine))
        def _():
            pltpu.make_async_copy(send_c.at[:, 0], send_c.at[:, 0], own_sem).wait()

    arrived(2, recv_c)
    yield

    spread = jnp.concatenate([tile(SPREAD + 64 * i, 64) for i in range(8)], 1)
    fold = jnp.concatenate([tile(FOLD, 128), tile(FOLD + 128, 128)], 1)
    whole = recv_c.reshape(256, 128)[...]
    for h in range(2):
        modes = []
        for c in range(2):
            first = c * 128 + h * 64
            modes.append(whole[first : first + 32].astype(F32) + whole[first + 32 : first + 64].astype(F32))
        mixed = stage_mix(
            jnp.concatenate(modes, 0).astype(BF),
            spread,
            fold,
            lambda r, p, q, lane: weight[r, p, 2 * h + q, :, lane : lane + 128],
        )
        send_d.reshape(128, 128)[h * 64 : h * 64 + 64] = mixed.astype(BF)

    @pl.loop(0, 32)
    def _(i):
        h = i & 1
        to = ((place + away(i >> 2)) & 7) * 2 + ((side + 1 + (i >> 1)) & 1)
        target_row = ((aisle + to) & 15) * 2 + h
        same = jnp.logical_and(target_row == row, to == aisle)

        @pl.when(same)
        def _():
            local(3, send_d.at[h, :, to & 7], recv_d.at[:, row])

        @pl.when(jnp.logical_not(same))
        def _():
            remote(3, send_d.at[h, :, to & 7], recv_d.at[:, row], (target_row, to))

    @ending.append
    def _():
        @pl.when(mine)
        def _():
            sent(3, recv_d.at[:, pl.ds(0, 31)])

        @pl.when(jnp.logical_not(mine))
        def _():
            sent(3, recv_d)

    arrived(3, recv_d)
    yield
    whole = recv_d.reshape(256, 128)[...]
    back = dot(tile(T23, 128)[:, 128:], jnp.concatenate([whole[:128], whole[128:]], 1)).astype(BF)
    for x in range(2):
        for o in range(2):
            i = 2 * x + o
            send_e.reshape(256, 128)[i * 64 : i * 64 + 64] = back[x * 64 : x * 64 + 64, o * 128 : o * 128 + 128]

    @pl.loop(0, NR - 1)
    def _(i):
        to = row_at(i)
        remote(4, send_e.at[:, to], recv_e.at[:, held], (to, aisle))

    local(4, send_e.at[:, row], recv_e.at[:, held])

    ending.append(lambda: sent(4, send_e.at[:, pl.ds(0, NR - 1)]))
    arrived(4, recv_e)
    yield
    whole = recv_e.reshape(256, 128)[...]
    back = stage_y_back([whole[i * 64 : i * 64 + 64] for i in range(4)], t4, pltpu.roll).astype(BF)
    for r in range(2):
        for o in range(2):
            part = back[r * 128 : r * 128 + 128, o * 128 : o * 128 + 128]
            send_f[:, r, o] = part.reshape(8, 16, 128)

    for step in (-2, -1, 1, 0):
        for other in (1, 0):
            to = aisle_at(step, other)
            if step or other:
                remote(5, send_f.at[to & 7], recv_f.at[group], (row, to))
    local(5, send_f.at[group], recv_f.at[group])

    ending.append(lambda: sent(5, send_f.at[pl.ds(0, 7)]))
    arrived(5, recv_f)
    yield
    planes = jnp.concatenate(
        [recv_f[:, 0].reshape(256, 128), recv_f[:, 1].reshape(256, 128)], 1
    )

    iz = [tile(IZ + 256 * i) for i in range(4)]

    def store(x, o, value):
        out[x, :, o * 16 : o * 16 + 16, :] = value

    stage_z_back(
        planes, tile(PERM), iz, lambda x, o: plain[x, :, o * 16 : o * 16 + 16, :], store
    )
    yield


def kernel(*refs):
    ending = []
    for _ in stages(*refs, ending):
        pass
    for wait in ending:
        wait()


def on_device(flow_state, mode_weight, bypass_weight, bias_term):
    hbm = pl.BlockSpec(memory_space=pltpu.HBM)
    pair = lambda *shape: [pltpu.VMEM(shape, BF)] * 2
    return pl.pallas_call(
        kernel,
        out_shape=pltpu.VMEM(flow_state.shape, BF),
        in_specs=[hbm] * 5,
        out_specs=pl.BlockSpec(memory_space=pltpu.VMEM),
        scratch_shapes=[
            pltpu.VMEM(flow_state.shape, BF),
            pltpu.VMEM(mode_weight.shape, BF),
            pltpu.VMEM(bypass_weight.shape, BF),
            pltpu.VMEM((1, C), F32),
            pltpu.VMEM((ROWS, 256), BF),
            *pair(8, 2, 16, 256),
            *pair(4, 32, 2, 128),
            *pair(2, 32, 4, 128),
            pltpu.VMEM((2, 2, 8, 4, 128), BF),
            pltpu.VMEM((2, 32, 4, 128), BF),
            *pair(4, 32, 2, 128),
            *pair(8, 2, 2, 16, 128),
            pltpu.VMEM((2, 16, 32, 256), F32),
            pltpu.SemaphoreType.DMA((6,)),
            pltpu.SemaphoreType.DMA((6,)),
            pltpu.SemaphoreType.DMA,
            pltpu.SemaphoreType.DMA((8,)),
        ],
        compiler_params=pltpu.CompilerParams(
            collective_id=0, has_side_effects=True, vmem_limit_bytes=60 * 2**20
        ),
        name="fourier_layer",
    )(flow_state, mode_weight, bypass_weight, bias_term.reshape(1, C), tables())


def solution(mesh):
    in_specs = (P("row", "aisle", None, None), P(None, "row", "aisle", None, None), P(), P())
    return jax.shard_map(
        on_device,
        mesh=mesh,
        in_specs=in_specs,
        out_specs=P("row", "aisle", None, None),
        check_vma=False,
    )
```

```python
import math

import jax
import jax.numpy as jnp
import numpy as np
from jax import lax
from jax.experimental import pallas as pl
from jax.experimental.pallas import tpu as pltpu
from jax.sharding import PartitionSpec as P

C = 32
MX = 64
MY = 64
MZ = 32
NX = 64
NY = 256
NZ = 256
NR = 32
NA = 16
SCALING = 1.0 / math.sqrt(NX * NY * NZ)
BF = jnp.bfloat16
F32 = jnp.float32
MESH = pl.DeviceIdType.MESH


def twiddle(frequencies, positions, length):
    phase = np.mod(frequencies[:, None] * positions[None, :], length).astype(np.float32)
    angles = phase * np.float32(2.0 * math.pi / length)
    return np.cos(angles), np.sin(angles)


def tables():
    cz, sz = twiddle(np.arange(MZ), np.arange(NZ), NZ)
    weight = np.where(np.arange(MZ) == 0, 1.0, 2.0).astype(np.float32)[:, None]
    forward = np.stack([cz, -sz], 0)
    inverse = np.stack([weight * cz, -weight * sz], 0)
    fz = np.zeros((2, 2, NZ, 2, 2, 2, MZ), np.float32)
    iz = np.zeros((2, 2, 2, 2, 2, MZ, NZ), np.float32)
    for x in range(2):
        for c in range(2):
            fz[x, c, :, :, c, x, :] = forward.transpose(2, 0, 1)
            iz[x, c, :, c, x] = inverse
    fz = fz.reshape(4, 256, 256)
    iz = iz.reshape(4, 256, 256)
    eye = np.eye(16, dtype=np.float32)
    perm = np.einsum("ab,cd->acdb", eye, eye).reshape(256, 256)
    cy, sy = twiddle(np.arange(MY) - MY // 2, np.arange(NY), NY)
    ty = np.stack([np.stack([cy, sy]), np.stack([-sy, cy])])
    t1 = ty.reshape(2, 2, 32, 2, 2, 128).transpose(4, 3, 2, 0, 1, 5).reshape(256, 256)
    cx, sx = twiddle(np.arange(MX) - MX // 2, np.arange(NX), NX)
    tx = np.stack([np.stack([cx, sx]), np.stack([-sx, cx])])
    t2 = tx.reshape(2, 2, MX, 32, 2).transpose(2, 0, 4, 3, 1).reshape(128, 128)
    bx = np.stack([np.stack([cx, -sx]), np.stack([sx, cx])])
    t3 = bx.reshape(2, 2, MX, 32, 2).transpose(4, 3, 0, 2, 1).reshape(128, 128)
    by = np.stack([np.stack([cy, -sy]), np.stack([sy, cy])])
    t4 = by.reshape(2, 2, 32, 2, 2, 128).transpose(0, 5, 4, 3, 2, 1).reshape(256, 256)
    spread = np.einsum("ab,ij,cd,o->iacdbjo", np.eye(8), np.eye(2), np.eye(4), np.ones(32))
    spread = spread.reshape(64, 2048)
    fold = np.einsum("lm,ab,ij,cd,g->liacdgmbj", np.eye(2), np.eye(8), np.eye(2), np.eye(4), np.ones(4))
    fold = fold.reshape(128, 512)
    halves = lambda t: np.concatenate(np.split(t, t.shape[1] // 256, 1), 0)
    packed = [
        fz.reshape(1024, 256),
        perm,
        t1,
        np.concatenate([t2, t3], 1),
        halves(spread),
        halves(fold),
        t4,
        iz.reshape(1024, 256),
    ]
    return jnp.asarray(np.concatenate(packed, 0), BF)


FZ = 0
PERM = 1024
T1 = 1280
T23 = 1536
SPREAD = 1664
FOLD = 2176
T4 = 2432
IZ = 2688
ROWS = 3712
GROUPS = ((FZ, T1), (T1, SPREAD), (SPREAD, T4), (T4, ROWS))


def dot(left, right):
    return jnp.dot(left, right, preferred_element_type=F32)


def dot_tn(left, right):
    return lax.dot_general(left, right, (((0,), (0,)), ((), ())), preferred_element_type=F32)


def dot_nt(left, right):
    return lax.dot_general(left, right, (((1,), (1,)), ((), ())), preferred_element_type=F32)


def exchange_halves(first, second, roll):
    low = (lax.broadcasted_iota(jnp.int32, first.shape, 1) & 32) == 0
    return (
        jnp.where(low, first, roll(second, 32, 1)),
        jnp.where(low, roll(first, 96, 1), second),
    )


def stage_z(flow, fz, perm):
    total = None
    for x in range(2):
        for c in range(2):
            part = dot(flow[x, :, c * 16 : c * 16 + 16, :].reshape(256, 256), fz[2 * x + c])
            total = part if total is None else total + part
    return dot(perm, total.astype(BF)).astype(BF)


def near(place, index):
    return ((index - place + 10) & 7) < 4


def near_tables(place, t1, t4):
    columns = (lax.broadcasted_iota(jnp.int32, (128, 256), 1) >> 5) & 3
    rows = (lax.broadcasted_iota(jnp.int32, (256, 128), 0) >> 5) & 3
    first, second = t1[:128].astype(F32), t1[128:].astype(F32)
    left, right = t4[:, :128].astype(F32), t4[:, 128:].astype(F32)
    return (
        jnp.where(near(place, columns), first, second).astype(BF),
        jnp.where(near(place, rows), left, right).astype(BF),
    )


def stage_y(gathered, t1, roll):
    wide = jnp.concatenate(gathered, 1)
    upper = jnp.concatenate([wide[:, 0:128], wide[:, 256:384]], 1)
    lower = jnp.concatenate([wide[:, 128:256], wide[:, 384:512]], 1)
    sums = dot(t1, jnp.concatenate([upper, lower], 0))
    parts = [
        exchange_halves(sums[:64, c * 128 : c * 128 + 128], sums[64:, c * 128 : c * 128 + 128], roll)
        for c in range(2)
    ]
    return [parts[c][x] for x in range(2) for c in range(2)]


def stage_mix(modes, spread, fold, weight):
    planes = []
    for p in range(2):
        wide = dot_tn(modes, spread[:, p * 1024 : p * 1024 + 1024])
        real = [None, None]
        imag = [None, None]
        for q in range(2):
            for c in range(2):
                rows = slice(c * 64 + q * 32, c * 64 + q * 32 + 32)
                for h in range(4):
                    mr = wide[rows, h * 128 : h * 128 + 128]
                    mi = wide[rows, 512 + h * 128 : 512 + h * 128 + 128]
                    wr = weight(0, p, q, c * 512 + h * 128)
                    wi = weight(1, p, q, c * 512 + h * 128)
                    re = mr * wr - mi * wi
                    im = mr * wi + mi * wr
                    real[q] = re if real[q] is None else real[q] + re
                    imag[q] = im if imag[q] is None else imag[q] + im
        planes += [jnp.concatenate(real, 0), jnp.concatenate(imag, 0)]
    total = jnp.concatenate(planes, 1)
    mixed = dot_nt(fold, total.astype(BF))
    return jnp.concatenate([mixed[:64], mixed[64:]], 1)


def stage_y_back(parts, t4, roll):
    columns = []
    for o in range(2):
        low, high = exchange_halves(parts[o].astype(F32), parts[2 + o].astype(F32), roll)
        columns.append(jnp.concatenate([low, high], 0).astype(BF))
    return dot(t4, jnp.concatenate(columns, 1))


def bypass_matrix(bypass, lanes):
    wide = dot(bypass, lanes).astype(BF)
    tall = jnp.concatenate([wide] * 8, 0)
    rows = lax.broadcasted_iota(jnp.int32, (256, 256), 0) // 32
    columns = lax.broadcasted_iota(jnp.int32, (256, 256), 1) // 32
    return jnp.where(rows == columns, tall, jnp.zeros_like(tall))


def stage_z_back(planes, perm, iz, bypass, store):
    rows = dot(perm, planes).astype(BF)
    for x in range(2):
        for o in range(2):
            spectral = dot(rows, iz[2 * x + o]) * SCALING
            total = spectral.reshape(16, 16, 256) + bypass(x, o)
            store(x, o, jax.nn.gelu(total).astype(BF))


def stages(
    flow_hbm, weight_hbm, bypass_hbm, bias_hbm, table_hbm,
    out,
    flow, weight, wide_weight, bypass, bias, table,
    send_a, recv_a, send_b, recv_b, send_c, recv_c, send_d, recv_d, send_e, recv_e, send_f, recv_f,
    plain, send_sem, recv_sem, own_sem, load_sem, ending,
):
    row = lax.axis_index("row")
    aisle = lax.axis_index("aisle")
    held = (row - 2 * aisle) & (NR - 1)
    quad = held >> 1
    half = row & 1
    place = aisle >> 1
    side = aisle & 1
    group = aisle & 7

    loads = [pltpu.make_async_copy(flow_hbm, flow, load_sem.at[0])]
    for i, (first, last) in enumerate(GROUPS):
        part = pl.ds(first, last - first)
        loads.append(pltpu.make_async_copy(table_hbm.at[part], table.at[part], load_sem.at[i + 1]))
    loads.append(pltpu.make_async_copy(bypass_hbm, bypass, load_sem.at[5]))
    loads.append(pltpu.make_async_copy(bias_hbm, bias, load_sem.at[6]))
    loads.append(pltpu.make_async_copy(weight_hbm, weight, load_sem.at[7]))
    barrier = pltpu.get_barrier_semaphore()

    def away(i):
        return (12 + ((i + 1) >> 1) * (1 - 2 * (i & 1))) & 7

    def row_at(i):
        low = ((row >> 4) + 1 + (i >> 1)) & 1
        return low * 16 + (((row >> 1) + away(i >> 2)) & 7) * 2 + ((row + 1 + i) & 1)

    def aisle_at(step, other):
        return ((place + step) & 7) * 2 + ((side + other) & 1)

    for step in (-3, -2, -1, 1, 0):
        for other in (1, 0):
            if step or other:
                to = aisle_at(step, other)
                pl.semaphore_signal(barrier, inc=1, device_id=(row, to), device_id_type=MESH)

    @pl.loop(0, NR - 1)
    def _(i):
        pl.semaphore_signal(barrier, inc=1, device_id=(row_at(i), aisle), device_id_type=MESH)

    for load in loads:
        load.start()

    def tile(first, rows=256):
        return table[first : first + rows]

    loads[0].wait()
    loads[1].wait()
    fz = [tile(FZ + 256 * i) for i in range(4)]
    send_a[...] = stage_z(flow, fz, tile(PERM)).reshape(8, 2, 16, 256)
    pl.semaphore_wait(barrier, 9 + NR - 1)

    def remote(stage, source, target, device):
        pltpu.make_async_remote_copy(
            src_ref=source,
            dst_ref=target,
            send_sem=send_sem.at[stage],
            recv_sem=recv_sem.at[stage],
            device_id=device,
            device_id_type=MESH,
        ).start()

    def local(stage, source, target):
        pltpu.make_async_copy(source, target, recv_sem.at[stage]).start()

    def arrived(stage, whole):
        pltpu.make_async_copy(whole, whole, recv_sem.at[stage]).wait()

    def sent(stage, part):
        pltpu.make_async_copy(part, part, send_sem.at[stage]).wait()

    for step in (2, -1, 1, 0):
        for other in (1, 0):
            to = aisle_at(step, other)
            if step or other:
                remote(0, send_a.at[to & 7], recv_a.at[group], (row, to))
    local(0, send_a.at[group], recv_a.at[group])

    ending.append(lambda: sent(0, send_a.at[pl.ds(0, 7)]))

    loads[5].wait()
    loads[6].wait()
    lanes = (
        lax.broadcasted_iota(jnp.int32, (32, 256), 0)
        == lax.broadcasted_iota(jnp.int32, (32, 256), 1) % 32
    ).astype(F32).astype(BF)
    diagonal = bypass_matrix(bypass[...], lanes)
    eye = lax.broadcasted_iota(jnp.int32, (32, 32), 0) == lax.broadcasted_iota(jnp.int32, (32, 32), 1)
    column = jnp.sum(jnp.where(eye, bias[...], 0.0), axis=1, keepdims=True)
    tall = jnp.concatenate([column] * 8, 0)
    for x in range(2):
        for y in range(2):
            field = flow[x, y * 8 : y * 8 + 8].reshape(256, 256)
            plain[x, y * 8 : y * 8 + 8] = (dot_tn(diagonal, field) + tall).reshape(8, 32, 256)

    for i in (2, 3, 4, 7):
        loads[i].wait()
    t1, t4 = near_tables(place, tile(T1), tile(T4))
    arrived(0, recv_a)
    yield
    parts = stage_y([recv_a[:, c].reshape(128, 256) for c in range(2)], t1, pltpu.roll)
    for i in range(4):
        send_b.reshape(256, 128)[i * 64 : i * 64 + 64] = parts[i].astype(BF)

    @pl.loop(0, NR - 1)
    def _(i):
        to = row_at(i)
        pair = (to - 2 * aisle) & (NR - 1)
        remote(1, send_b.at[:, pair], recv_b.at[:, row], (to, aisle))

    local(1, send_b.at[:, held], recv_b.at[:, row])

    ending.append(lambda: sent(1, send_b.at[:, pl.ds(0, NR - 1)]))
    arrived(1, recv_b)
    yield
    whole = recv_b.reshape(256, 128)[...]
    columns = [jnp.concatenate([whole[c * 64 : c * 64 + 64], whole[128 + c * 64 : 192 + c * 64]], 0) for c in range(2)]
    modes = (dot(tile(T23, 128)[:, :128], jnp.concatenate(columns, 1)) * SCALING).astype(BF)
    for c in range(2):
        send_c.reshape(256, 128)[c * 128 : c * 128 + 128] = modes[:, c * 128 : c * 128 + 128]

    mine = quad == aisle
    slot = half * 16 + aisle

    @pl.loop(0, NR - 1)
    def _(i):
        to = row_at(i)
        remote(2, send_c.at[:, to], recv_c.at[:, slot], (to, quad))

    @pl.when(mine)
    def _():
        local(2, send_c.at[:, row], recv_c.at[:, slot])

    @pl.when(jnp.logical_not(mine))
    def _():
        pltpu.make_async_remote_copy(
            src_ref=send_c.at[:, row],
            dst_ref=recv_c.at[:, slot],
            send_sem=own_sem,
            recv_sem=recv_sem.at[2],
            device_id=(row, quad),
            device_id_type=MESH,
        ).start()

    ending.append(lambda: sent(2, send_c.at[:, pl.ds(0, NR - 1)]))
    @ending.append
    def _():
        @pl.when(jnp.logical_not(mine))
        def _():
            pltpu.make_async_copy(send_c.at[:, 0], send_c.at[:, 0], own_sem).wait()

    wide_weight[...] = weight[...].astype(F32)
    arrived(2, recv_c)
    yield

    spread = jnp.concatenate([tile(SPREAD + 64 * i, 64) for i in range(8)], 1)
    fold = jnp.concatenate([tile(FOLD, 128), tile(FOLD + 128, 128)], 1)
    whole = recv_c.reshape(256, 128)[...]
    for h in range(2):
        modes = []
        for c in range(2):
            first = c * 128 + h * 64
            modes.append(whole[first : first + 32].astype(F32) + whole[first + 32 : first + 64].astype(F32))
        mixed = stage_mix(
            jnp.concatenate(modes, 0).astype(BF),
            spread,
            fold,
            lambda r, p, q, lane: wide_weight[r, p, 2 * h + q, :, lane : lane + 128],
        )
        send_d.reshape(128, 128)[h * 64 : h * 64 + 64] = mixed.astype(BF)

    @pl.loop(0, 32)
    def _(i):
        h = i & 1
        to = ((place + away(i >> 2)) & 7) * 2 + ((side + 1 + (i >> 1)) & 1)
        target_row = ((aisle + to) & 15) * 2 + h
        same = jnp.logical_and(target_row == row, to == aisle)

        @pl.when(same)
        def _():
            local(3, send_d.at[h, :, to & 7], recv_d.at[:, row])

        @pl.when(jnp.logical_not(same))
        def _():
            remote(3, send_d.at[h, :, to & 7], recv_d.at[:, row], (target_row, to))

    @ending.append
    def _():
        @pl.when(mine)
        def _():
            sent(3, recv_d.at[:, pl.ds(0, 31)])

        @pl.when(jnp.logical_not(mine))
        def _():
            sent(3, recv_d)

    arrived(3, recv_d)
    yield
    whole = recv_d.reshape(256, 128)[...]
    back = dot(tile(T23, 128)[:, 128:], jnp.concatenate([whole[:128], whole[128:]], 1)).astype(BF)
    for x in range(2):
        for o in range(2):
            i = 2 * x + o
            send_e.reshape(256, 128)[i * 64 : i * 64 + 64] = back[x * 64 : x * 64 + 64, o * 128 : o * 128 + 128]

    @pl.loop(0, NR - 1)
    def _(i):
        to = row_at(i)
        remote(4, send_e.at[:, to], recv_e.at[:, held], (to, aisle))

    local(4, send_e.at[:, row], recv_e.at[:, held])

    ending.append(lambda: sent(4, send_e.at[:, pl.ds(0, NR - 1)]))
    arrived(4, recv_e)
    yield
    whole = recv_e.reshape(256, 128)[...]
    back = stage_y_back([whole[i * 64 : i * 64 + 64] for i in range(4)], t4, pltpu.roll).astype(BF)
    for r in range(2):
        for o in range(2):
            part = back[r * 128 : r * 128 + 128, o * 128 : o * 128 + 128]
            send_f[:, r, o] = part.reshape(8, 16, 128)

    for step in (-2, -1, 1, 0):
        for other in (1, 0):
            to = aisle_at(step, other)
            if step or other:
                remote(5, send_f.at[to & 7], recv_f.at[group], (row, to))
    local(5, send_f.at[group], recv_f.at[group])

    ending.append(lambda: sent(5, send_f.at[pl.ds(0, 7)]))
    arrived(5, recv_f)
    yield
    planes = jnp.concatenate(
        [recv_f[:, 0].reshape(256, 128), recv_f[:, 1].reshape(256, 128)], 1
    )

    iz = [tile(IZ + 256 * i) for i in range(4)]

    def store(x, o, value):
        out[x, :, o * 16 : o * 16 + 16, :] = value

    stage_z_back(
        planes, tile(PERM), iz, lambda x, o: plain[x, :, o * 16 : o * 16 + 16, :], store
    )
    yield


def kernel(*refs):
    ending = []
    for _ in stages(*refs, ending):
        pass
    for wait in ending:
        wait()


def on_device(flow_state, mode_weight, bypass_weight, bias_term):
    hbm = pl.BlockSpec(memory_space=pltpu.HBM)
    pair = lambda *shape: [pltpu.VMEM(shape, BF)] * 2
    return pl.pallas_call(
        kernel,
        out_shape=pltpu.VMEM(flow_state.shape, BF),
        in_specs=[hbm] * 5,
        out_specs=pl.BlockSpec(memory_space=pltpu.VMEM),
        scratch_shapes=[
            pltpu.VMEM(flow_state.shape, BF),
            pltpu.VMEM(mode_weight.shape, BF),
            pltpu.VMEM(mode_weight.shape, F32),
            pltpu.VMEM(bypass_weight.shape, BF),
            pltpu.VMEM((1, C), F32),
            pltpu.VMEM((ROWS, 256), BF),
            *pair(8, 2, 16, 256),
            *pair(4, 32, 2, 128),
            *pair(2, 32, 4, 128),
            pltpu.VMEM((2, 2, 8, 4, 128), BF),
            pltpu.VMEM((2, 32, 4, 128), BF),
            *pair(4, 32, 2, 128),
            *pair(8, 2, 2, 16, 128),
            pltpu.VMEM((2, 16, 32, 256), F32),
            pltpu.SemaphoreType.DMA((6,)),
            pltpu.SemaphoreType.DMA((6,)),
            pltpu.SemaphoreType.DMA,
            pltpu.SemaphoreType.DMA((8,)),
        ],
        compiler_params=pltpu.CompilerParams(
            collective_id=0, has_side_effects=True, vmem_limit_bytes=60 * 2**20
        ),
        name="fourier_layer",
    )(flow_state, mode_weight, bypass_weight, bias_term.reshape(1, C), tables())


def solution(mesh):
    in_specs = (P("row", "aisle", None, None), P(None, "row", "aisle", None, None), P(), P())
    return jax.shard_map(
        on_device,
        mesh=mesh,
        in_specs=in_specs,
        out_specs=P("row", "aisle", None, None),
        check_vma=False,
    )
```
